128 devices in a mesh: lat: 8 (over x, core), lon: 8 (over y_lo, z), tp: 2 (over y_hi).
Axes of the slice: x: 4, y: 4 (y_hi: 2, y_lo: 2; y = y_hi * 2 + y_lo), z: 4, core: 2. Of those that a mesh axis runs over, the one named last changes fastest.
Arguments:
- patches: bfloat16 [4, 192, 192, 512], P(None, 'lat', ('lon', 'tp')), may hold values from -6 to 6
- region_ids: int32 [4, 192, 192], P(None, 'lat', ('lon', 'tp')), may hold values from 0 to 3
- triple_one: bfloat16 [512, 3, 512], replicated, may hold values from -0.25 to 0.25
- output_one: bfloat16 [512, 512], replicated, may hold values from -0.25 to 0.25
- expand_one: bfloat16 [512, 2048], replicated, may hold values from -0.25 to 0.25
- shrink_one: bfloat16 [2048, 512], replicated, may hold values from -0.125 to 0.125
- scales_one: bfloat16 [8], replicated, may hold values from 4 to 16
- merge_weight: bfloat16 [2048, 1024], replicated, may hold values from -0.125 to 0.125
- triple_two: bfloat16 [1024, 3, 1024], P('tp'), may hold values from -0.1875 to 0.1875
- output_two: bfloat16 [1024, 1024], P('tp'), may hold values from -0.1875 to 0.1875
- expand_two: bfloat16 [4096, 1024], P('tp'), may hold values from -0.1875 to 0.1875
- shrink_two: bfloat16 [4096, 1024], P('tp'), may hold values from -0.09375 to 0.09375
- scales_two: bfloat16 [16], P('tp'), may hold values from 4 to 16
Outputs:
- skip: bfloat16 [4, 192, 192, 512], P(None, 'lat', ('lon', 'tp'))
- coarse: bfloat16 [4, 96, 96, 1024], P(None, 'lat', ('lon', 'tp'))
The draws below stay inside these ranges and needn't reach their ends.
All inputs are finite; a program needn't handle non-finite values.
Results may differ from the reference program's by a relative error of at most 0.024.
Values may be sent and summed in bfloat16 or wider, within the bound.
No kernel may reach another device: no remote copies, remote signals or barrier semaphores. Data moves between devices by JAX's collectives and lax.ppermute only.
A program may use at most 192 MiB of HBM per device.

```python
import math
import jax
import jax.numpy as jnp
from jax import lax

WIDTH_ONE = 512
HEADS_ONE = 8
HIDDEN_ONE = 2048
WIDTH_TWO = 1024
HEADS_TWO = 16
HIDDEN_TWO = 4096
LEVELS = 4
WIN_LEV = 2
WIN_LAT = 6
WIN_LON = 12
NLAT = 192
NLON = 192


def with_ends(drawn, stream_key, low, high):
    place = [jax.random.randint(jax.random.fold_in(stream_key, axis), (), 0, length) for axis, length in enumerate(drawn.shape)]
    widest = drawn.shape.index(max(drawn.shape))
    neighbour = place[:widest] + [(place[widest] + 1) % drawn.shape[widest]] + place[widest + 1:]
    return drawn.at[tuple(place)].set(low).at[tuple(neighbour)].set(high)


def shard_levels(own_key, dims, cuts, smallest, largest):
    gain, own = 1.0, jax.random.fold_in(own_key, 6)
    for dim, shards_of in cuts:
        draws = jnp.exp(jax.random.uniform(jax.random.fold_in(own, dim), (shards_of,), jnp.float32, smallest / len(cuts), largest / len(cuts)))
        gain = gain * jnp.repeat(draws, dims[dim] // shards_of).reshape([-1 if axis == dim else 1 for axis in range(len(dims))])
    return gain


def noise(stream_key, extent, deviation, most, shards=(), held_as=jnp.bfloat16):
    level = shard_levels(stream_key, extent, shards, -0.22, 0.18) if shards else 1.0
    drawn = jax.random.normal(stream_key, extent, jnp.float32) * deviation * level
    return jnp.minimum(jnp.maximum(drawn, -most), most).astype(held_as)


def setup_inputs(seed: int = 0) -> dict:
    key_of = jax.random.split(jax.random.key(seed), 14)
    patches = noise(key_of[0], (LEVELS, NLAT, NLON, WIDTH_ONE), 1.0, 6.0, ((1, 8), (2, 16)))
    region_ids = with_ends(jax.random.randint(key_of[1], (LEVELS, NLAT, NLON), 0, 4), jax.random.fold_in(key_of[1], 1), 0, 3).astype(jnp.int32)
    triple_one = noise(key_of[2], (WIDTH_ONE, 3, WIDTH_ONE), WIDTH_ONE ** -0.5, 0.25)
    output_one = noise(key_of[3], (WIDTH_ONE, WIDTH_ONE), WIDTH_ONE ** -0.5, 0.25)
    expand_one = noise(key_of[4], (WIDTH_ONE, HIDDEN_ONE), WIDTH_ONE ** -0.5, 0.25)
    shrink_one = noise(key_of[5], (HIDDEN_ONE, WIDTH_ONE), HIDDEN_ONE ** -0.5, 0.125)
    scales_one = jnp.clip(jnp.exp(jax.random.uniform(key_of[6], (HEADS_ONE,), jnp.float32, math.log(4.0), math.log(16.0))), 4.0, 16.0).astype(jnp.bfloat16)
    merge_weight = noise(key_of[7], (4 * WIDTH_ONE, WIDTH_TWO), (4 * WIDTH_ONE) ** -0.5, 0.125)
    triple_two = noise(key_of[8], (WIDTH_TWO, 3, WIDTH_TWO), WIDTH_TWO ** -0.5, 0.1875, ((0, 2),))
    output_two = noise(key_of[9], (WIDTH_TWO, WIDTH_TWO), WIDTH_TWO ** -0.5, 0.1875, ((0, 2),))
    expand_two = noise(key_of[10], (HIDDEN_TWO, WIDTH_TWO), WIDTH_TWO ** -0.5, 0.1875, ((0, 2),))
    shrink_two = noise(key_of[11], (HIDDEN_TWO, WIDTH_TWO), HIDDEN_TWO ** -0.5, 0.09375, ((0, 2),))
    scales_two = jnp.clip(jnp.exp(math.log(16.0) - 1.3862944 * jax.random.uniform(key_of[12], (HEADS_TWO,), jnp.float32) ** shard_levels(key_of[12], (HEADS_TWO,), ((0, 2),), -0.2, 0.2)), 4.0, 16.0).astype(jnp.bfloat16)
    return dict(patches=patches, region_ids=region_ids, triple_one=triple_one, output_one=output_one, expand_one=expand_one, shrink_one=shrink_one, scales_one=scales_one, merge_weight=merge_weight, triple_two=triple_two, output_two=output_two, expand_two=expand_two, shrink_two=shrink_two, scales_two=scales_two)


def layer_norm(values):
    row_mean = lax.optimization_barrier(jnp.mean(values, axis=-1, keepdims=True))
    centred = values - row_mean
    spread = lax.optimization_barrier(jnp.mean(centred * centred, axis=-1, keepdims=True))
    return centred * lax.rsqrt(spread + 1e-05)

def to_windows(blocks):
    levels, lat_rows, lon_cols = blocks.shape[:3]
    trailing = blocks.shape[3:]
    shaped = blocks.reshape((levels // WIN_LEV, WIN_LEV, lat_rows // WIN_LAT, WIN_LAT, lon_cols // WIN_LON, WIN_LON) + trailing)
    axes_order = (0, 2, 4, 1, 3, 5) + tuple(range(6, 6 + len(trailing)))
    return shaped.transpose(axes_order).reshape((-1, WIN_LEV * WIN_LAT * WIN_LON) + trailing)

def from_windows(windows, levels, lat_rows, lon_cols):
    trailing = windows.shape[2:]
    shaped = windows.reshape((levels // WIN_LEV, lat_rows // WIN_LAT, lon_cols // WIN_LON, WIN_LEV, WIN_LAT, WIN_LON) + trailing)
    axes_order = (0, 3, 1, 4, 2, 5) + tuple(range(6, 6 + len(trailing)))
    return shaped.transpose(axes_order).reshape((levels, lat_rows, lon_cols) + trailing)

def unit_rows(vectors):
    widened = vectors.astype(jnp.float32)
    return (widened * lax.rsqrt(lax.optimization_barrier(jnp.sum(widened * widened, axis=-1, keepdims=True)) + 1e-06)).astype(jnp.bfloat16)

def window_attention(windows, triple, scales, window_ids):
    win_count, win_points, in_width = windows.shape
    head_count = scales.shape[0]
    head_size = triple.shape[0] // head_count
    flat_tokens = windows.reshape(win_count * win_points, in_width)
    packed = jnp.einsum('ti,jci->tcj', flat_tokens.astype(jnp.float32), triple.astype(jnp.float32)).astype(jnp.bfloat16)
    packed = packed.reshape(win_count, win_points, 3, head_count, head_size)
    queries = unit_rows(packed[:, :, 0])
    keyrows = unit_rows(packed[:, :, 1])
    valrows = packed[:, :, 2]
    scores = jnp.einsum('wqhd,wkhd->whqk', queries.astype(jnp.float32), keyrows.astype(jnp.float32))
    scores = scores * scales.astype(jnp.float32)[None, :, None, None]
    weights = jnp.exp(scores)
    if window_ids is not None:
        allowed = window_ids[:, None, :, None] == window_ids[:, None, None, :]
        weights = jnp.where(allowed, weights, jnp.float32(0.0))
    shares = (weights / lax.optimization_barrier(jnp.sum(weights, axis=-1, keepdims=True))).astype(jnp.bfloat16)
    attended = jnp.einsum('whqk,wkhd->wqhd', shares.astype(jnp.float32), valrows.astype(jnp.float32)).astype(jnp.bfloat16)
    return attended.reshape(win_count * win_points, head_count * head_size)

def section_one(windows, window_ids, triple_one, output_one, expand_one, shrink_one, scales_one):
    flat_tokens = windows.reshape(-1, windows.shape[-1])
    attended = window_attention(windows, triple_one, scales_one, window_ids)
    branch = jnp.dot(attended, output_one, preferred_element_type=jnp.float32)
    hidden = (flat_tokens.astype(jnp.float32) + layer_norm(branch)).astype(jnp.bfloat16)
    expanded = jax.nn.gelu(jnp.dot(hidden, expand_one, preferred_element_type=jnp.float32)).astype(jnp.bfloat16)
    shrunk = jnp.dot(expanded, shrink_one, preferred_element_type=jnp.float32)
    result = (hidden.astype(jnp.float32) + layer_norm(shrunk)).astype(jnp.bfloat16)
    return result.reshape(windows.shape)

def merge_patches(skip, merge_weight):
    levels, lat_rows, lon_cols, feature_count = skip.shape
    quartets = skip.reshape(levels, lat_rows // 2, 2, lon_cols // 2, 2, feature_count)
    quartets = quartets.transpose(0, 1, 3, 2, 4, 5).reshape(levels * (lat_rows // 2) * (lon_cols // 2), 4 * feature_count)
    normed = layer_norm(quartets.astype(jnp.float32)).astype(jnp.bfloat16)
    merged = jnp.dot(normed, merge_weight, preferred_element_type=jnp.float32).astype(jnp.bfloat16)
    return merged.reshape(levels, lat_rows // 2, lon_cols // 2, merge_weight.shape[1])

def reference(patches, region_ids, triple_one, output_one, expand_one, shrink_one, scales_one, merge_weight, triple_two, output_two, expand_two, shrink_two, scales_two):
    shifts = (WIN_LEV // 2, WIN_LAT // 2, WIN_LON // 2)
    shifted = jnp.roll(patches, (-shifts[0], -shifts[1], -shifts[2]), axis=(0, 1, 2))
    windows = to_windows(shifted)
    window_ids = to_windows(region_ids)
    groups = LEVELS // WIN_LEV
    grouped = windows.reshape((groups, -1) + windows.shape[1:])
    grouped_ids = window_ids.reshape((groups, -1) + window_ids.shape[1:])

    def one_group(pair_args):
        return section_one(pair_args[0], pair_args[1], triple_one, output_one, expand_one, shrink_one, scales_one)
    finished = lax.map(one_group, (grouped, grouped_ids))
    unrolled = from_windows(finished.reshape(windows.shape), LEVELS, NLAT, NLON)
    skip = jnp.roll(unrolled, shifts, axis=(0, 1, 2))
    coarse_in = merge_patches(skip, merge_weight)
    windows_two = to_windows(coarse_in)
    flat_two = windows_two.reshape(-1, WIDTH_TWO)
    attended = window_attention(windows_two, triple_two, scales_two, None)
    branch = jnp.dot(attended, output_two, preferred_element_type=jnp.float32)
    hidden = (flat_two.astype(jnp.float32) + layer_norm(branch)).astype(jnp.bfloat16)
    expanded = jax.nn.gelu(jnp.einsum('ti,hi->th', hidden.astype(jnp.float32), expand_two.astype(jnp.float32))).astype(jnp.bfloat16)
    shrunk = jnp.dot(expanded, shrink_two, preferred_element_type=jnp.float32)
    result = (hidden.astype(jnp.float32) + layer_norm(shrunk)).astype(jnp.bfloat16)
    coarse = from_windows(result.reshape(windows_two.shape[:2] + (WIDTH_TWO,)), LEVELS, NLAT // 2, NLON // 2)
    return (skip, coarse)
```

```python
import math

import jax
import jax.numpy as jnp
import numpy as np
from jax import lax
from jax.experimental import pallas as pl
from jax.experimental.pallas import tpu as pltpu
from jax.sharding import PartitionSpec as P

BF = jnp.bfloat16
F32 = jnp.float32
MASK = 192.0
LOG2E = math.log2(math.e)
MIB = 1024 * 1024


def home_level(lg, l):
    return (2 * lg + l + 1) % 4


def pack_interior():
    mat = np.zeros((288, 384), np.float32)
    for half in range(2):
        for lg in range(2):
            for i in range(6):
                for l in range(2):
                    for j in range(6):
                        row = half * 144 + lg * 72 + i * 12 + l * 6 + j
                        mat[row, (home_level(lg, l) * 6 + i) * 16 + half * 6 + j] = 1
    return mat


def pack_edge():
    mat = np.zeros((144, 192), np.float32)
    for half in range(2):
        for lg in range(2):
            for i in range(3):
                for l in range(2):
                    for j in range(6):
                        row = half * 72 + lg * 36 + i * 12 + l * 6 + j
                        mat[row, (home_level(lg, l) * 3 + i) * 16 + half * 6 + j] = 1
    return mat


def unpack_edges():
    mat = np.zeros((384, 288), np.float32)
    edge = pack_edge()
    for e in range(2):
        for half in range(2):
            mat[e * 192:(e + 1) * 192, half * 144 + e * 72:half * 144 + e * 72 + 72] = edge[
                half * 72:half * 72 + 72
            ].T
    return mat


def merge_rows():
    mat = np.zeros((2, 4, 144, 864), np.float32)
    for g in range(2):
        for m in range(4):
            pi, pj = m // 2, m % 2
            for lg2 in range(2):
                for l2 in range(2):
                    level = lg2 * 2 + l2
                    lg, l = ((level - 1) % 4) // 2, ((level - 1) % 4) % 2
                    for ii in range(6):
                        i = 2 * (6 * g + ii) + pi
                        for jj in range(6):
                            half, j = jj // 3, 2 * (jj % 3) + pj
                            if i < 3 or i >= 21:
                                edge, ie = (0, i) if i < 3 else (1, i - 21)
                                col = half * 144 + edge * 72 + lg * 36 + ie * 12 + l * 6 + j
                            else:
                                w, iw = (i - 3) // 6, (i - 3) % 6
                                col = 288 * (w + 1 - g) + half * 144 + lg * 72 + iw * 12 + l * 6 + j
                            mat[g, m, lg2 * 72 + l2 * 36 + ii * 6 + jj, col] = 1
    return mat.reshape(2, 576, 864)


def coarse_rows():
    mat = np.zeros((192, 144), np.float32)
    for level in range(4):
        for ii in range(6):
            for jj in range(6):
                row = (level * 6 + ii) * 8 + jj
                mat[row, (level // 2) * 72 + (level % 2) * 36 + ii * 6 + jj] = 1
    return mat


def const(mat):
    return jnp.asarray(mat, dtype=BF)


def dot(a, b):
    return lax.dot_general(a, b, (((1,), (0,)), ((), ())), preferred_element_type=F32)


def dot_nt(a, b):
    return lax.dot_general(a, b, (((1,), (1,)), ((), ())), preferred_element_type=F32)


def normed(values):
    centred = values - jnp.mean(values, axis=-1, keepdims=True)
    spread = jnp.mean(centred * centred, axis=-1, keepdims=True)
    return centred * lax.rsqrt(spread + 1e-05)


def gelu(x):
    inner = x * (0.7978845608028654 + 0.035677408136300125 * (x * x))
    return (0.5 * x) * (1.0 + jnp.tanh(inner))


def unit(packed, ones, factor=None):
    wide = packed.astype(F32)
    squares = (wide * wide).astype(BF)
    total = jnp.concatenate([dot(squares[:, :256], ones), dot(squares[:, 256:], ones)], axis=1)
    result = wide * lax.rsqrt(total + 1e-06)
    if factor is not None:
        result = result * factor
    return result.astype(BF)


def heads(q, k, v, lanes, aug_q=None, aug_k=None):
    low, high = lanes[0:1], lanes[1:2]
    parts = []
    for pair in range(4):
        span = slice(pair * 128, pair * 128 + 128)
        qp, kp, vp = q[:, span], k[:, span], v[:, span]
        if aug_q is not None:
            qp = jnp.concatenate([qp, aug_q], axis=1)
        acc = None
        for sel in (low, high):
            ks = kp * sel
            if aug_k is not None:
                ks = jnp.concatenate([ks, aug_k], axis=1)
            weights = jnp.exp2(dot_nt(qp, ks)).astype(BF)
            values = jnp.concatenate([vp * sel, jnp.broadcast_to(sel, vp.shape)], axis=1)
            term = dot(weights, values)
            acc = term if acc is None else acc + term
        parts.append(acc[:, :128] / acc[:, 128:])
    return jnp.concatenate(parts, axis=1).astype(BF)


def full(ref):
    return ref[...]


def call(kernel, outs, args, flops, vmem=40, smem=(), scratch=()):
    specs = [
        pl.BlockSpec(memory_space=pltpu.SMEM if n in smem else pltpu.VMEM) for n in range(len(args))
    ]
    moved = sum(int(np.prod(a.shape)) * a.dtype.itemsize for a in args)
    return pl.pallas_call(
        kernel,
        out_shape=[jax.ShapeDtypeStruct(shape, kind) for shape, kind in outs],
        in_specs=specs,
        out_specs=[pl.BlockSpec(memory_space=pltpu.VMEM) for _ in outs],
        scratch_shapes=list(scratch),
        compiler_params=pltpu.CompilerParams(vmem_limit_bytes=vmem * MIB),
        cost_estimate=pl.CostEstimate(flops=flops, bytes_accessed=moved, transcendentals=0),
    )(*args)


def pack_kernel(x, pint, pedge, ltop, rtop, lbot, rbot, l01, r01, l2, r2):
    def rows(start, count):
        block = x[:, start:start + count]
        pad = jnp.zeros((4, count, 4, 512), BF)
        return jnp.concatenate([block, pad], axis=2).reshape(4 * count * 16, 512)

    for start, left, right in ((0, ltop, rtop), (21, lbot, rbot)):
        got = dot(pedge[...], rows(start, 3))
        left[...] = got[:72].astype(BF)
        right[...] = got[72:].astype(BF)
    for w, (left, right, at) in enumerate(((l01, r01, 0), (l01, r01, 144), (l2, r2, 0))):
        got = dot(pint[...], rows(3 + 6 * w, 6))
        left[at:at + 144] = got[:144].astype(BF)
        right[at:at + 144] = got[144:].astype(BF)


def interior_kernel(xr, xl, aug_q, aug_k, w3, out, ones, lanes, srow, hr, hl):
    count = xr.shape[0] // 144
    for n in range(count):
        right = xr[n * 144:n * 144 + 144].astype(F32)
        left = xl[n * 144:n * 144 + 144].astype(F32)
        wide = jnp.concatenate([right[:72], left[:72], right[72:], left[72:]], axis=0)
        x = wide.astype(BF)
        q = unit(dot_nt(x, w3[0]).astype(BF), ones[...], srow[...])
        k = unit(dot_nt(x, w3[1]).astype(BF), ones[...])
        v = dot_nt(x, w3[2]).astype(BF)
        att = []
        for lg in range(2):
            span = slice(lg * 144, lg * 144 + 144)
            aug = slice(n * 288 + lg * 144, n * 288 + lg * 144 + 144)
            att.append(heads(q[span], k[span], v[span], lanes[...], aug_q[aug], aug_k[aug]))
        branch = dot(jnp.concatenate(att, axis=0), out[...])
        hid = wide + normed(branch)
        hr[n * 144:n * 144 + 144] = jnp.concatenate([hid[:72], hid[144:216]], axis=0).astype(BF)
        hl[n * 144:n * 144 + 144] = jnp.concatenate([hid[72:144], hid[216:]], axis=0).astype(BF)


def edges_kernel(
    rtop, ltop, ertop, eltop, rbot, lbot, erbot, elbot, aug_q, aug_k, w3, out, ones, lanes, srow, hr, hl
):
    hids = []
    for e, (r, l, er, el) in enumerate(((rtop, ltop, ertop, eltop), (rbot, lbot, erbot, elbot))):
        wide = jnp.concatenate([r[...].astype(F32), l[...].astype(F32)], axis=0)
        ext = jnp.concatenate([er[...].astype(F32), el[...].astype(F32)], axis=0)
        both = jnp.concatenate([wide, ext], axis=0).astype(BF)
        q = unit(dot_nt(both[:144], w3[0]).astype(BF), ones[...], srow[...])
        k = unit(dot_nt(both, w3[1]).astype(BF), ones[...])
        v = dot_nt(both, w3[2]).astype(BF)
        att = heads(
            q, k, v, lanes[...], aug_q[e * 144:e * 144 + 144], aug_k[e * 288:e * 288 + 288]
        )
        hids.append(wide + normed(dot(att, out[...])))
    hr[...] = jnp.concatenate([hids[0][:72], hids[1][:72]], axis=0).astype(BF)
    hl[...] = jnp.concatenate([hids[0][72:], hids[1][72:]], axis=0).astype(BF)


def feed_one(h, expand, shrink):
    acc = None
    for c in range(4):
        span = slice(c * 512, c * 512 + 512)
        grown = gelu(dot(h, expand[:, span])).astype(BF)
        term = dot(grown, shrink[span, :])
        acc = term if acc is None else acc + term
    return (h.astype(F32) + normed(acc)).astype(BF)


def feed_kernel(a, b, c, expand, shrink, oa, ob, oc):
    for src, dst in ((a, oa), (b, ob), (c, oc)):
        for at in range(0, src.shape[0], 144):
            dst[at:at + 144] = feed_one(src[at:at + 144], expand, shrink)


def merge_kernel(l01, l2, le, r01, r2, re, pm, weight, c0, c1, ball):
    ball[0:144] = le[...]
    ball[144:288] = re[...]
    for w, (l, r, at) in enumerate(((l01, r01, 0), (l01, r01, 144), (l2, r2, 0))):
        ball[288 * w + 288:288 * w + 432] = l[at:at + 144]
        ball[288 * w + 432:288 * w + 576] = r[at:at + 144]
    for g, dst in ((0, c0), (1, c1)):
        picked = dot(pm[g, :, 0:288], ball[0:288]) + dot(
            pm[g, :, 288:864], ball[288 + 288 * g:864 + 288 * g]
        )
        quartet = jnp.concatenate([picked[m * 144:m * 144 + 144] for m in range(4)], axis=1)
        dst[...] = dot(normed(quartet).astype(BF), weight[...]).astype(BF)


def skip_kernel(l01, l2, le, r01, r2, re, pint, pedges, skip):
    both = jnp.concatenate([le[...], re[...]], axis=0)
    got = dot(pedges[...], both).reshape(2, 4, 3, 16, 512)[:, :, :, :12].astype(BF)
    skip[:, 0:3] = got[0]
    skip[:, 21:24] = got[1]
    for w, (l, r, at) in enumerate(((l01, r01, 0), (l01, r01, 144), (l2, r2, 0))):
        both = jnp.concatenate([l[at:at + 144], r[at:at + 144]], axis=0)
        got = dot(pint[...], both).reshape(4, 6, 16, 512)[:, :, :12].astype(BF)
        skip[:, 3 + 6 * w:9 + 6 * w] = got


def attend_two_kernel(me, own, other, w3, ones, lanes, srow, x_out, att_out):
    a, b = own[...].astype(F32), other[...].astype(F32)
    first = me[0] == 0
    t0, t1 = jnp.where(first, a, b), jnp.where(first, b, a)
    x = jnp.concatenate([t0[:72], t1[:72], t0[72:], t1[72:]], axis=0).astype(BF)
    x_out[...] = x
    q = unit(dot_nt(x, w3[0]).astype(BF), ones[...], srow[...])
    k = unit(dot_nt(x, w3[1]).astype(BF), ones[...])
    v = dot_nt(x, w3[2]).astype(BF)
    for lg in range(2):
        span = slice(lg * 144, lg * 144 + 144)
        att_out[span] = heads(q[span], k[span], v[span], lanes[...])


def feed_two_kernel(me, x, mine, theirs, o_mine, o_theirs, expand, shrink, keep, send, hid_own):
    branch = dot(mine[...], o_mine[...]) + dot(theirs[...], o_theirs[...])
    hid = (x[...].astype(F32) + normed(branch)).astype(BF)
    acc = None
    for c in range(4):
        span = slice(c * 512, c * 512 + 512)
        grown = gelu(dot_nt(hid, expand[span, :])).astype(BF)
        term = dot(grown, shrink[span, :])
        acc = term if acc is None else acc + term
    first = me[0] == 0

    def split(values):
        p0 = jnp.concatenate([values[0:72], values[144:216]], axis=0)
        p1 = jnp.concatenate([values[72:144], values[216:288]], axis=0)
        return jnp.where(first, p0, p1), jnp.where(first, p1, p0)

    own, far = split(acc)
    keep[...] = own
    send[...] = far.astype(BF)
    hid_own[...] = split(hid.astype(F32))[0].astype(BF)


def finish_kernel(k0, k1, r0, r1, h0, h1, pout, coarse):
    for g, (k, r, h) in enumerate(((k0, r0, h0), (k1, r1, h1))):
        done = (h[...].astype(F32) + normed(k[...] + r[...].astype(F32))).astype(BF)
        got = dot(pout[...], done).reshape(4, 6, 8, 1024)[:, :, :6].astype(BF)
        coarse[:, 6 * g:6 * g + 6] = got


def behind(value, axis, steps):
    count = lax.axis_size(axis)
    return lax.ppermute(value, axis, [(s, (s + steps) % count) for s in range(count)])


def classes(ids, steps):
    lane = lax.broadcasted_iota(jnp.int32, ids.shape + (128,), ids.ndim)
    hit = ids[..., None] == lane
    for_q = jnp.where(hit, MASK, jnp.where(lane == 8, -MASK, 0.0)).astype(BF)
    for_k = jnp.where(hit | (lane == 8), 1.0, 0.0).astype(BF)
    return for_q, for_k


def shards(
    patches,
    region_ids,
    triple_one,
    output_one,
    expand_one,
    shrink_one,
    scales_one,
    merge_weight,
    triple_two,
    output_two,
    expand_two,
    shrink_two,
    scales_two,
):
    lat_at = lax.axis_index("lat")
    me = lax.axis_index("tp").astype(jnp.int32).reshape(1)
    pint, pedge = pack_interior(), pack_edge()
    ones = const(np.kron(np.eye(4), np.ones((64, 64))))
    lane_of = np.zeros((8, 128), np.float32)
    lane_of[0, :64] = 1
    lane_of[1, 64:] = 1
    lanes = const(lane_of)
    col_axes = ("lon", "tp")

    eighth = lax.dynamic_slice_in_dim(output_two, lat_at * 64, 64, axis=0)
    o_theirs = lax.all_gather(behind(eighth, "tp", 1), "lat", axis=0, tiled=True)

    tok = lambda n: ((n, 512), BF)
    ltop, rtop, lbot, rbot, l01, r01, l2, r2 = call(
        pack_kernel,
        [tok(72), tok(72), tok(72), tok(72), tok(288), tok(288), tok(144), tok(144)],
        [patches, const(pint), const(pedge)],
        10**9,
    )
    ltop, lbot = behind(ltop, col_axes, -1), behind(lbot, col_axes, -1)
    l01, l2 = behind(l01, col_axes, -1), behind(l2, col_axes, -1)
    ertop, erbot = behind(rbot, "lat", 1), behind(rtop, "lat", -1)
    eltop, elbot = behind(lbot, "lat", 1), behind(ltop, "lat", -1)

    ids = region_ids.reshape(2, 2, 4, 6, 2, 6).transpose(2, 0, 4, 3, 1, 5)
    inner = ids[:3].reshape(3 * 288)
    last = ids[3].transpose(1, 0, 2, 3, 4) + 4 * jnp.arange(2, dtype=jnp.int32)[None, :, None, None, None]
    prev = behind(last, "lat", 1)
    bottom = [last[:, :, :3].reshape(144), last[:, :, 3:].reshape(144)]
    top = [prev[:, :, 3:].reshape(144), prev[:, :, :3].reshape(144)]
    in_q, in_k = classes(inner, 0)
    edge_q, edge_k = classes(jnp.concatenate(top + bottom), 0)
    edge_q = jnp.concatenate([edge_q[:144], edge_q[288:432]], axis=0)

    w_one = triple_one.transpose(1, 0, 2)
    s_one = jnp.repeat(scales_one.astype(F32) * LOG2E, 64)[None, :]
    shared = [w_one, output_one, ones, lanes, s_one]
    hr01, hl01 = call(
        interior_kernel,
        [tok(288), tok(288)],
        [r01, l01, in_q[:576], in_k[:576]] + shared,
        2 * 10**9,
    )
    hl01 = behind(hl01, col_axes, 1)
    hr2, hl2 = call(
        interior_kernel, [tok(144), tok(144)], [r2, l2, in_q[576:], in_k[576:]] + shared, 10**9
    )
    hl2 = behind(hl2, col_axes, 1)
    hre, hle = call(
        edges_kernel,
        [tok(144), tok(144)],
        [rtop, ltop, ertop, eltop, rbot, lbot, erbot, elbot, edge_q, edge_k] + shared,
        2 * 10**9,
    )
    hle = behind(hle, col_axes, 1)
    trio = [tok(288), tok(144), tok(144)]
    br = call(feed_kernel, trio, [hr01, hr2, hre, expand_one, shrink_one], 3 * 10**9)
    bl = call(feed_kernel, trio, [hl01, hl2, hle, expand_one, shrink_one], 3 * 10**9)
    blocks = list(bl) + list(br)
    c0, c1 = call(
        merge_kernel,
        [((144, 1024), BF)] * 2,
        blocks + [const(merge_rows()), merge_weight],
        3 * 10**9,
        scratch=[pltpu.VMEM((1152, 512), BF)],
    )
    d0, d1 = behind(c0, "tp", 1), behind(c1, "tp", 1)
    skip = call(
        skip_kernel,
        [((4, 24, 12, 512), BF)],
        blocks + [const(pint.T), const(unpack_edges())],
        10**9,
    )[0]

    w_two = triple_two.transpose(1, 0, 2)
    s_two = jnp.repeat(scales_two.astype(F32) * LOG2E, 64)[None, :]
    attended = []
    for own, other in ((c0, d0), (c1, d1)):
        x, mine = call(
            attend_two_kernel,
            [((288, 1024), BF), tok(288)],
            [me, own, other, w_two, ones, lanes, s_two],
            2 * 10**9,
            smem=(0,),
        )
        attended.append((x, mine, behind(mine, "tp", 1)))
    kept = []
    for x, mine, theirs in attended:
        keep, send, hid_own = call(
            feed_two_kernel,
            [((144, 1024), F32), ((144, 1024), BF), ((144, 1024), BF)],
            [me, x, mine, theirs, output_two, o_theirs, expand_two, shrink_two],
            4 * 10**9,
            smem=(0,),
        )
        kept.append((keep, behind(send, "tp", 1), hid_own))
    (k0, g0, h0), (k1, g1, h1) = kept
    coarse = call(
        finish_kernel,
        [((4, 12, 6, 1024), BF)],
        [k0, k1, g0, g1, h0, h1, const(coarse_rows())],
        10**9,
    )[0]
    return (skip, coarse)


def solution(mesh):
    in_specs = (
        P(None, "lat", ("lon", "tp"), None),
        P(None, "lat", ("lon", "tp")),
        P(),
        P(),
        P(),
        P(),
        P(),
        P(),
        P("tp", None, None),
        P("tp", None),
        P("tp", None),
        P("tp", None),
        P("tp"),
    )
    out_specs = (P(None, "lat", ("lon", "tp"), None), P(None, "lat", ("lon", "tp"), None))
    return jax.shard_map(shards, mesh=mesh, in_specs=in_specs, out_specs=out_specs, check_vma=False)
```

```python
import functools
import math

import jax
import jax.numpy as jnp
import numpy as np
from jax import lax
from jax.experimental import pallas as pl
from jax.experimental.pallas import tpu as pltpu
from jax.sharding import PartitionSpec as P

BF = jnp.bfloat16
F32 = jnp.float32
MASK = 192.0
LOG2E = math.log2(math.e)
MIB = 1024 * 1024


def home_level(lg, l):
    return (2 * lg + l + 1) % 4


def pick_rows():
    rows, keep = np.zeros((1152, 48), np.float32), np.zeros((1152, 24), np.float32)
    group = np.zeros((1152, 1), np.float32)
    at = 0
    for w in range(4):
        for part in range(2 if w == 3 else 1):
            outer = [(h, g) for h in range(2) for g in range(2)]
            if w < 3:
                outer = [(h, g) for g in range(2) for h in range(2)]
            for half, lg in outer:
                for l in range(2):
                    for i in range(3 * part, 3 * part + 3) if w == 3 else range(6):
                        for j in range(6):
                            rows[at, (half * 6 + j) * 4 + 2 * lg + l] = 1
                            keep[at, 6 * w + i] = 1
                            group[at] = 4 * lg
                            at += 1
    return rows, np.concatenate([keep, group], axis=1)


def place(level, i, j):
    lg, l = ((level - 1) % 4) // 2, ((level - 1) % 4) % 2
    if i < 3 or i >= 21:
        edge, ie = (0, i) if i < 3 else (1, i - 21)
        return edge * 72 + lg * 36 + l * 18 + ie * 6 + j
    w, iw = (i - 3) // 6, (i - 3) % 6
    return 144 + w * 144 + lg * 72 + l * 36 + iw * 6 + j


def home_rows():
    mat = np.zeros((576, 576), np.float32)
    for level in range(4):
        for j in range(6):
            for i in range(24):
                mat[level * 144 + j * 24 + i, place(level, i, j)] = 1
    return mat


def merge_rows():
    mat = np.zeros((2, 4, 144, 864), np.float32)
    for g in range(2):
        for m in range(4):
            pi, pj = m // 2, m % 2
            for level in range(4):
                for ii in range(6):
                    i = 2 * (6 * g + ii) + pi
                    for jj in range(6):
                        half, j = jj // 3, 2 * (jj % 3) + pj
                        at = place(level, i, j)
                        chunk = 0 if at < 144 else at // 144 - g
                        row = (level // 2) * 72 + (level % 2) * 36 + ii * 6 + jj
                        mat[g, m, row, 288 * chunk + half * 144 + at % 144] = 1
    return mat.reshape(2, 576, 864)


def coarse_rows():
    mat = np.zeros((144, 144), np.float32)
    for level in range(4):
        for ii in range(6):
            for jj in range(6):
                row = (ii * 6 + jj) * 4 + level
                mat[row, (level // 2) * 72 + (level % 2) * 36 + ii * 6 + jj] = 1
    return mat


def const(mat):
    return jnp.asarray(mat, dtype=BF)


def dot(a, b):
    return lax.dot_general(a, b, (((1,), (0,)), ((), ())), preferred_element_type=F32)


def dot_nt(a, b):
    return lax.dot_general(a, b, (((1,), (1,)), ((), ())), preferred_element_type=F32)


def normed(values):
    centred = values - jnp.mean(values, axis=-1, keepdims=True)
    spread = jnp.mean(centred * centred, axis=-1, keepdims=True)
    return centred * lax.rsqrt(spread + 1e-05)


def gelu(x):
    inner = x * (0.7978845608028654 + 0.035677408136300125 * (x * x))
    return (0.5 * x) * (1.0 + jnp.tanh(inner))


def unit(packed, ones, factor=None):
    wide = packed.astype(F32)
    squares = (wide * wide).astype(BF)
    total = jnp.concatenate([dot(squares[:, :256], ones), dot(squares[:, 256:], ones)], axis=1)
    result = wide * lax.rsqrt(total + 1e-06)
    if factor is not None:
        result = result * factor
    return result.astype(BF)


def heads(q, k, v, lanes, aug_q=None, aug_k=None):
    count = q.shape[0]
    low, high = lanes[0:1], lanes[1:2]
    first = lax.broadcasted_iota(jnp.int32, (count, 128), 1) < 64
    if aug_q is not None:
        aug_q = jnp.concatenate([aug_q, aug_q], axis=0)
    ones = jnp.ones((v.shape[0], 128), BF)
    parts = []
    for pair in range(4):
        span = slice(pair * 128, pair * 128 + 128)
        qp, kp = q[:, span], k[:, span]
        qp = jnp.concatenate([qp * low, qp * high], axis=0)
        if aug_q is not None:
            qp = jnp.concatenate([qp, aug_q], axis=1)
            kp = jnp.concatenate([kp, aug_k], axis=1)
        weights = jnp.exp2(dot_nt(qp, kp)).astype(BF)
        acc = dot(weights, jnp.concatenate([v[:, span], ones], axis=1))
        both = jnp.where(first, acc[:count, :128], acc[count:, :128])
        total = jnp.where(first, acc[:count, 128:], acc[count:, 128:])
        parts.append(both / total)
    return jnp.concatenate(parts, axis=1).astype(BF)


def call(kernel, outs, args, flops, vmem=16, smem=(), hbm=(), scratch=()):
    def space(n):
        return pltpu.SMEM if n in smem else pltpu.HBM if n in hbm else pltpu.VMEM

    moved = sum(int(np.prod(a.shape)) * a.dtype.itemsize for a in args)
    return pl.pallas_call(
        kernel,
        out_shape=[jax.ShapeDtypeStruct(shape, kind) for shape, kind in outs],
        in_specs=[pl.BlockSpec(memory_space=space(n)) for n in range(len(args))],
        out_specs=[pl.BlockSpec(memory_space=pltpu.VMEM) for _ in outs],
        scratch_shapes=list(scratch),
        compiler_params=pltpu.CompilerParams(vmem_limit_bytes=vmem * MIB),
        cost_estimate=pl.CostEstimate(flops=flops, bytes_accessed=moved, transcendentals=0),
    )(*args)


def pack_kernel(x, left, right):
    row = lax.broadcasted_iota(jnp.int32, (144, 144), 0)
    col = lax.broadcasted_iota(jnp.int32, (144, 144), 1)
    six = (row * 10923) >> 16
    lat = jnp.where(row < 18, six, jnp.where(row < 36, six + 18, six - 3))
    perm = jnp.where(col == (row - 6 * six) * 24 + lat, 1.0, 0.0).astype(BF)
    for half, dst in enumerate((left, right)):
        got = []
        for level in (1, 2, 3, 0):
            at = level * 288 + half * 144
            got.append(dot(perm, x[at:at + 144]))
        rows = [g[e:e + 18] for e in (0, 18) for g in got]
        dst[:144] = jnp.concatenate(rows, axis=0).astype(BF)
        rows = [g[w:w + 36] for w in (36, 72, 108) for g in got]
        dst[144:] = jnp.concatenate(rows, axis=0).astype(BF)


def ready_kernel(
    at, ids, rows, keep, sone, stwo, spread, o_two, classes, s_one, s_two, quarter, sem
):
    copy = pltpu.make_async_copy(
        o_two.at[pl.ds(pl.multiple_of(at[0] * 128, 128), 128)], quarter, sem
    )
    copy.start()
    for src, dst in ((sone, s_one), (stwo, s_two)):
        dst[...] = dot(src[...], spread[...])[0:1] * LOG2E
    grid = jnp.concatenate([ids[c] for c in range(12)], axis=0).astype(F32).astype(BF)
    picked = jnp.concatenate([dot(rows[...], grid), jnp.ones((1152, 1), F32)], axis=1)
    name = jnp.sum(picked * keep[...].astype(F32), axis=1, keepdims=True)
    lane = lax.broadcasted_iota(jnp.int32, (1152, 128), 1)
    hit = (lane.astype(F32) == name) | (lane == 8)
    classes[...] = jnp.where(hit, 1.0, 0.0).astype(BF)
    copy.wait()


def rim_kernel(left_all, right_all, classes, down, up):
    left, right = left_all[:144].astype(F32), right_all[:144].astype(F32)
    marks = classes[864:].astype(F32)
    up[...] = jnp.concatenate([right[:72], left[:72]], axis=0).astype(BF)
    wide = jnp.concatenate([marks[b * 72:b * 72 + 72] for b in range(4)], axis=1)
    down[...] = jnp.concatenate([right[72:], left[72:], wide], axis=0).astype(BF)


def join_kernel(at, a, b, c, d, out):
    mine = at[0]
    for step, part in enumerate((a, b, c, d)):
        out[pl.ds(pl.multiple_of((mine ^ step) * 128, 128), 128)] = part[...]


def windows_of(right, left):
    parts = []
    for at in range(0, right.shape[0], 72):
        parts += [right[at:at + 72], left[at:at + 72]]
    return jnp.concatenate(parts, axis=0)


def halves_of(rows):
    right = [rows[at:at + 72] for at in range(0, rows.shape[0], 144)]
    left = [rows[at + 72:at + 144] for at in range(0, rows.shape[0], 144)]
    return jnp.concatenate(right, axis=0).astype(BF), jnp.concatenate(left, axis=0).astype(BF)


def project(x, w3, ones, srow, first=None):
    q = unit(dot_nt(x[:first], w3[0]).astype(BF), ones[...], srow[...])
    k = unit(dot_nt(x, w3[1]).astype(BF), ones[...])
    return q, k, dot_nt(x, w3[2]).astype(BF)


def first_kernel(right, left, classes, w3, out, ones, lanes, srow, hr, hl):
    wide = windows_of(right[144:432].astype(F32), left[144:432].astype(F32))
    q, k, v = project(wide.astype(BF), w3, ones, srow)
    att = []
    for at in range(0, 576, 144):
        span = slice(at, at + 144)
        mark = classes[span]
        att.append(heads(q[span], k[span], v[span], lanes[...], mark * lanes[2:3], mark))
    hr[...], hl[...] = halves_of(wide + normed(dot(jnp.concatenate(att, axis=0), out[...])))


def second_kernel(right_all, left_all, down, up, classes, w3, out, ones, lanes, srow, hr, hl):
    right, left = (
        jnp.concatenate([ref[432:].astype(F32), ref[:144].astype(F32)], axis=0)
        for ref in (right_all, left_all)
    )
    wide = windows_of(right, left)
    x = jnp.concatenate([wide.astype(BF), down[:144], up[...]], axis=0)
    q, k, v = project(x, w3, ones, srow, 576)
    got = down[144:216]
    far = jnp.concatenate([got[:, b * 128:b * 128 + 128].astype(F32) for b in range(4)], axis=0)
    far = far.astype(BF)
    att = []
    for at in (0, 144):
        span = slice(at, at + 144)
        mark = classes[576 + at:720 + at]
        att.append(heads(q[span], k[span], v[span], lanes[...], mark * lanes[2:3], mark))
    marks = (jnp.concatenate([far[144:], far[:144]], axis=0), classes[864:1152])
    for e in range(2):
        own, ext = slice(288 + e * 144, 432 + e * 144), slice(576 + e * 144, 720 + e * 144)
        keys = jnp.concatenate([k[own], k[ext]], axis=0)
        values = jnp.concatenate([v[own], v[ext]], axis=0)
        att.append(
            heads(q[own], keys, values, lanes[...], marks[e][:144] * lanes[2:3], marks[e])
        )
    hr[...], hl[...] = halves_of(wide + normed(dot(jnp.concatenate(att, axis=0), out[...])))


def feed_one(h, expand, shrink):
    acc = None
    for c in range(4):
        span = slice(c * 512, c * 512 + 512)
        grown = gelu(dot(h, expand[:, span])).astype(BF)
        term = dot(grown, shrink[span, :])
        acc = term if acc is None else acc + term
    return (h.astype(F32) + normed(acc)).astype(BF)


def feed_kernel(h1, h2, expand, shrink, out1, out2):
    got = feed_one(jnp.concatenate([h1[...], h2[...]], axis=0), expand, shrink)
    out1[...] = got[:288]
    out2[...] = got[288:]


def feed_some_kernel(h, expand, shrink, out):
    out[...] = feed_one(h[...], expand, shrink)


def merge_kernel(l1, l2, r1, r2, pm, weight, coarse, ball, *, g):
    for half, (one, two) in enumerate(((l1, l2), (r1, r2))):
        for n, block in enumerate((two[144:], (one[:144], one[144:])[g], (one[144:], two[:144])[g])):
            ball[288 * n + half * 144:288 * n + half * 144 + 144] = block
    picked = dot(pm[g], ball[...])
    quartet = jnp.concatenate([picked[m * 144:m * 144 + 144] for m in range(4)], axis=1)
    coarse[...] = dot(normed(quartet).astype(BF), weight[...]).astype(BF)


def skip_kernel(l1, l2, r1, r2, perm, skip):
    for half, (one, two) in enumerate(((l1, l2), (r1, r2))):
        own = jnp.concatenate([two[144:], one[...], two[:144]], axis=0)
        got = dot(perm[...], own).astype(BF)
        for l in range(4):
            at = l * 288 + half * 144
            skip[at:at + 144] = got[l * 144:l * 144 + 144]


def attend_two_kernel(me, own, other, w3, ones, lanes, srow, x_out, att_out):
    a, b = own[...].astype(F32), other[...].astype(F32)
    first = me[0] == 0
    t0, t1 = jnp.where(first, a, b), jnp.where(first, b, a)
    x = jnp.concatenate([t0[:72], t1[:72], t0[72:], t1[72:]], axis=0).astype(BF)
    x_out[...] = x
    q = unit(dot_nt(x, w3[0]).astype(BF), ones[...], srow[...])
    k = unit(dot_nt(x, w3[1]).astype(BF), ones[...])
    v = dot_nt(x, w3[2]).astype(BF)
    for lg in range(2):
        span = slice(lg * 144, lg * 144 + 144)
        att_out[span] = heads(q[span], k[span], v[span], lanes[...])


def feed_two_kernel(me, x, mine, theirs, o_mine, o_theirs, expand, shrink, keep, send, hid_own):
    branch = dot(mine[...], o_mine[...]) + dot(theirs[...], o_theirs[...])
    hid = (x[...].astype(F32) + normed(branch)).astype(BF)
    acc = None
    for c in range(4):
        span = slice(c * 512, c * 512 + 512)
        grown = gelu(dot_nt(hid, expand[span, :])).astype(BF)
        term = dot(grown, shrink[span, :])
        acc = term if acc is None else acc + term
    first = me[0] == 0

    def split(values):
        p0 = jnp.concatenate([values[0:72], values[144:216]], axis=0)
        p1 = jnp.concatenate([values[72:144], values[216:288]], axis=0)
        return jnp.where(first, p0, p1), jnp.where(first, p1, p0)

    own, far = split(acc)
    keep[...] = own
    send[...] = far.astype(BF)
    hid_own[...] = split(hid.astype(F32))[0].astype(BF)


def finish_rows(k, r, h, pout):
    done = (h[...].astype(F32) + normed(k[...] + r[...].astype(F32))).astype(BF)
    return dot(pout[...], done).reshape(6, 6, 4, 1024).astype(BF)


def finish_first_kernel(k, r, h, pout, rows):
    rows[...] = finish_rows(k, r, h, pout)


def finish_kernel(first, k, r, h, pout, coarse):
    coarse[:6] = first[...]
    coarse[6:] = finish_rows(k, r, h, pout)


def behind(value, axis, steps):
    count = lax.axis_size(axis)
    return lax.ppermute(value, axis, [(s, (s + steps) % count) for s in range(count)])


def after(value, done):
    return lax.optimization_barrier((value, done))[0]


def across(value, axis, flip):
    return lax.ppermute(value, axis, [(s, s ^ flip) for s in range(lax.axis_size(axis))])


def shards(
    patches,
    region_ids,
    triple_one,
    output_one,
    expand_one,
    shrink_one,
    scales_one,
    merge_weight,
    triple_two,
    output_two,
    expand_two,
    shrink_two,
    scales_two,
):
    me = lax.axis_index("tp").astype(jnp.int32).reshape(1)
    lat_at = (lax.axis_index("lat") & 3).astype(jnp.int32).reshape(1)
    ones = const(np.kron(np.eye(4), np.ones((64, 64))))
    lane_of = np.zeros((8, 128), np.float32)
    lane_of[0, :64] = 1
    lane_of[1, 64:] = 1
    lane_of[2] = MASK
    lane_of[2, 8] = -MASK
    lanes = const(lane_of)
    spread = const(np.kron(np.eye(8), np.ones((1, 64))))
    col_axes = ("lon", "tp")
    tok = lambda n: ((n, 512), BF)

    flat = patches.transpose(0, 2, 1, 3).reshape(1152, 512)
    left, right = call(
        pack_kernel,
        [tok(576)] * 2,
        [flat],
        10**9,
    )
    region_ids = after(region_ids, right)
    left = behind(left, col_axes, -1)
    pick, keep = pick_rows()
    classes, s_one, s_two, quarter = call(
        ready_kernel,
        [((1152, 128), BF), ((1, 512), F32), ((1, 512), F32), ((128, 1024), BF)],
        [
            lat_at,
            region_ids.transpose(2, 0, 1),
            const(pick),
            const(keep),
            scales_one.reshape(1, 8),
            scales_two.reshape(1, 8),
            spread,
            output_two,
        ],
        10**9,
        smem=(0,),
        hbm=(7,),
        scratch=[pltpu.SemaphoreType.DMA],
    )
    quarter = after(quarter, left)
    oa = behind(quarter, "tp", 1)
    down, up = call(rim_kernel, [tok(216), tok(144)], [left, right, classes], 10**6)
    classes = after(classes, down)
    down, up = behind(down, "lat", 1), behind(up, "lat", -1)

    w_one = triple_one.transpose(1, 0, 2)
    shared = [classes, w_one, output_one, ones, lanes, s_one]
    hr1, hl1 = call(first_kernel, [tok(288)] * 2, [right, left] + shared, 4 * 10**9)
    hl1 = behind(hl1, col_axes, 1)
    shared[0] = after(classes, hr1)
    hr2, hl2 = call(
        second_kernel, [tok(288)] * 2, [right, left, down, up] + shared, 6 * 10**9
    )
    hl2 = behind(hl2, col_axes, 1)

    feeds = [expand_one, shrink_one]
    br1, br2 = call(feed_kernel, [tok(288)] * 2, [hr1, hr2] + feeds, 3 * 10**9)
    oa = after(oa, br1)
    ob, oc = across(oa, "lat", 1), across(oa, "lat", 2)
    bl1 = call(feed_some_kernel, [tok(288)], [after(hl1, br1)] + feeds, 2 * 10**9)[0]
    bl2 = call(feed_some_kernel, [tok(288)], [after(hl2, bl1)] + feeds, 2 * 10**9)[0]
    blocks = [bl1, bl2, br1, br2]
    od = across(after(oc, bl2), "lat", 1)
    pm, coarse_in = const(merge_rows()), []
    for g in range(2):
        if g:
            blocks = [after(blocks[0], coarse_in[0])] + blocks[1:]
        coarse_in += call(
            functools.partial(merge_kernel, g=g),
            [((144, 1024), BF)],
            blocks + [pm, merge_weight],
            10**9,
            scratch=[pltpu.VMEM((864, 512), BF)],
        )
    c0, c1 = coarse_in
    d0, d1 = behind(c0, "tp", 1), behind(c1, "tp", 1)
    blocks[0], od = after(blocks[0], c1), after(od, c1)
    skip = call(skip_kernel, [tok(1152)], blocks + [const(home_rows())], 2 * 10**9)[0]
    o_theirs = call(
        join_kernel, [((512, 1024), BF)], [lat_at, oa, ob, oc, od], 10**9, smem=(0,)
    )[0]
    c0, skip, o_theirs = lax.optimization_barrier((c0, skip, o_theirs))
    skip = skip.reshape(4, 12, 24, 512).transpose(0, 2, 1, 3)

    w_two = triple_two.transpose(1, 0, 2)
    attended = []
    for own, other in ((c0, d0), (c1, d1)):
        if attended:
            own = after(own, attended[0][1])
        x, mine = call(
            attend_two_kernel,
            [((288, 1024), BF), tok(288)],
            [me, own, other, w_two, ones, lanes, s_two],
            2 * 10**9,
            smem=(0,),
        )
        attended.append((x, mine, behind(mine, "tp", 1)))
    kept = []
    for x, mine, theirs in attended:
        if kept:
            x = after(x, kept[0][0])
        keep, send, hid_own = call(
            feed_two_kernel,
            [((144, 1024), F32), ((144, 1024), BF), ((144, 1024), BF)],
            [me, x, mine, theirs, output_two, o_theirs, expand_two, shrink_two],
            10**8,
            smem=(0,),
        )
        kept.append((keep, behind(send, "tp", 1), hid_own))
    pout = const(coarse_rows())
    first = call(finish_first_kernel, [((6, 6, 4, 1024), BF)], [*kept[0], pout], 10**8)[0]
    coarse = call(finish_kernel, [((12, 6, 4, 1024), BF)], [first, *kept[1], pout], 10**8)[0]
    return (skip, coarse.transpose(2, 0, 1, 3))


def solution(mesh):
    in_specs = (
        P(None, "lat", ("lon", "tp"), None),
        P(None, "lat", ("lon", "tp")),
        P(),
        P(),
        P(),
        P(),
        P(),
        P(),
        P("tp", None, None),
        P("tp", None),
        P("tp", None),
        P("tp", None),
        P("tp"),
    )
    out_specs = (P(None, "lat", ("lon", "tp"), None), P(None, "lat", ("lon", "tp"), None))
    return jax.shard_map(shards, mesh=mesh, in_specs=in_specs, out_specs=out_specs, check_vma=False)
```

```python
import functools
import math

import jax
import jax.numpy as jnp
import numpy as np
from jax import lax
from jax.experimental import pallas as pl
from jax.experimental.pallas import tpu as pltpu
from jax.sharding import PartitionSpec as P

BF = jnp.bfloat16
F32 = jnp.float32
MASK = 192.0
LOG2E = math.log2(math.e)
MIB = 1024 * 1024


def home_level(lg, l):
    return (2 * lg + l + 1) % 4


def pick_rows():
    rows, keep = np.zeros((1152, 48), np.float32), np.zeros((1152, 24), np.float32)
    group = np.zeros((1152, 1), np.float32)
    at = 0
    for w in range(4):
        for part in range(2 if w == 3 else 1):
            outer = [(h, g) for h in range(2) for g in range(2)]
            if w < 3:
                outer = [(h, g) for g in range(2) for h in range(2)]
            for half, lg in outer:
                for l in range(2):
                    for i in range(3 * part, 3 * part + 3) if w == 3 else range(6):
                        for j in range(6):
                            rows[at, (half * 6 + j) * 4 + 2 * lg + l] = 1
                            keep[at, 6 * w + i] = 1
                            group[at] = 4 * lg
                            at += 1
    return rows, np.concatenate([keep, group], axis=1)


def place(level, i, j):
    lg, l = ((level - 1) % 4) // 2, ((level - 1) % 4) % 2
    if i < 3 or i >= 21:
        edge, ie = (0, i) if i < 3 else (1, i - 21)
        return edge * 72 + lg * 36 + l * 18 + ie * 6 + j
    w, iw = (i - 3) // 6, (i - 3) % 6
    return 144 + w * 144 + lg * 72 + l * 36 + iw * 6 + j


def home_rows():
    mat = np.zeros((576, 576), np.float32)
    for level in range(4):
        for j in range(6):
            for i in range(24):
                mat[level * 144 + j * 24 + i, place(level, i, j)] = 1
    return mat


def merge_rows():
    mat = np.zeros((2, 4, 144, 864), np.float32)
    for g in range(2):
        for m in range(4):
            pi, pj = m // 2, m % 2
            for level in range(4):
                for ii in range(6):
                    i = 2 * (6 * g + ii) + pi
                    for jj in range(6):
                        half, j = jj // 3, 2 * (jj % 3) + pj
                        at = place(level, i, j)
                        chunk = 0 if at < 144 else at // 144 - g
                        row = (level // 2) * 72 + (level % 2) * 36 + ii * 6 + jj
                        mat[g, m, row, 288 * chunk + half * 144 + at % 144] = 1
    return mat.reshape(2, 576, 864)


def coarse_rows():
    mat = np.zeros((144, 144), np.float32)
    for level in range(4):
        for ii in range(6):
            for jj in range(6):
                row = (ii * 6 + jj) * 4 + level
                mat[row, (level // 2) * 72 + (level % 2) * 36 + ii * 6 + jj] = 1
    return mat


def const(mat):
    return jnp.asarray(mat, dtype=BF)


def dot(a, b):
    return lax.dot_general(a, b, (((1,), (0,)), ((), ())), preferred_element_type=F32)


def dot_nt(a, b):
    return lax.dot_general(a, b, (((1,), (1,)), ((), ())), preferred_element_type=F32)


def normed(values):
    centred = values - jnp.mean(values, axis=-1, keepdims=True)
    spread = jnp.mean(centred * centred, axis=-1, keepdims=True)
    return centred * lax.rsqrt(spread + 1e-05)


def gelu(x):
    inner = x * (0.7978845608028654 + 0.035677408136300125 * (x * x))
    return (0.5 * x) * (1.0 + jnp.tanh(inner))


def unit(packed, ones, factor=None):
    wide = packed.astype(F32)
    squares = (wide * wide).astype(BF)
    total = jnp.concatenate([dot(squares[:, :256], ones), dot(squares[:, 256:], ones)], axis=1)
    result = wide * lax.rsqrt(total + 1e-06)
    if factor is not None:
        result = result * factor
    return result.astype(BF)


def heads(q, k, v, lanes, aug_q=None, aug_k=None):
    count = q.shape[0]
    low, high = lanes[0:1], lanes[1:2]
    first = lax.broadcasted_iota(jnp.int32, (count, 128), 1) < 64
    if aug_q is not None:
        aug_q = jnp.concatenate([aug_q, aug_q], axis=0)
    ones = jnp.ones((v.shape[0], 128), BF)
    parts = []
    for pair in range(4):
        span = slice(pair * 128, pair * 128 + 128)
        qp, kp = q[:, span], k[:, span]
        qp = jnp.concatenate([qp * low, qp * high], axis=0)
        if aug_q is not None:
            qp = jnp.concatenate([qp, aug_q], axis=1)
            kp = jnp.concatenate([kp, aug_k], axis=1)
        weights = jnp.exp2(dot_nt(qp, kp)).astype(BF)
        acc = dot(weights, jnp.concatenate([v[:, span], ones], axis=1))
        both = jnp.where(first, acc[:count, :128], acc[count:, :128])
        total = jnp.where(first, acc[:count, 128:], acc[count:, 128:])
        parts.append(both / total)
    return jnp.concatenate(parts, axis=1).astype(BF)


def call(kernel, outs, args, flops, vmem=16, smem=(), hbm=(), scratch=()):
    def space(n):
        return pltpu.SMEM if n in smem else pltpu.HBM if n in hbm else pltpu.VMEM

    moved = sum(int(np.prod(a.shape)) * a.dtype.itemsize for a in args)
    return pl.pallas_call(
        kernel,
        out_shape=[jax.ShapeDtypeStruct(shape, kind) for shape, kind in outs],
        in_specs=[pl.BlockSpec(memory_space=space(n)) for n in range(len(args))],
        out_specs=[pl.BlockSpec(memory_space=pltpu.VMEM) for _ in outs],
        scratch_shapes=list(scratch),
        compiler_params=pltpu.CompilerParams(vmem_limit_bytes=vmem * MIB),
        cost_estimate=pl.CostEstimate(flops=flops, bytes_accessed=moved, transcendentals=0),
    )(*args)


def pack_kernel(x, out):
    row = lax.broadcasted_iota(jnp.int32, (144, 144), 0)
    col = lax.broadcasted_iota(jnp.int32, (144, 144), 1)
    six = (row * 10923) >> 16
    lat = jnp.where(row < 18, six, jnp.where(row < 36, six + 18, six - 3))
    perm = jnp.where(col == (row - 6 * six) * 24 + lat, 1.0, 0.0).astype(BF)
    got = [dot(perm, x[level]) for level in (1, 2, 3, 0)]
    rows = [g[e:e + 18] for e in (0, 18) for g in got]
    out[:144] = jnp.concatenate(rows, axis=0).astype(BF)
    rows = [g[w:w + 36] for w in (36, 72, 108) for g in got]
    out[144:] = jnp.concatenate(rows, axis=0).astype(BF)


def ready_kernel(
    at, ids, rows, keep, sone, stwo, spread, o_two, classes, s_one, s_two, part, sem
):
    copy = pltpu.make_async_copy(
        o_two.at[pl.ds(pl.multiple_of(at[0] * 128, 128), 128)], part, sem
    )
    copy.start()
    for src, dst in ((sone, s_one), (stwo, s_two)):
        dst[...] = dot(src[...], spread[...])[0:1] * LOG2E
    grid = jnp.concatenate([ids[c] for c in range(12)], axis=0).astype(F32).astype(BF)
    picked = jnp.concatenate([dot(rows[...], grid), jnp.ones((1152, 1), F32)], axis=1)
    name = jnp.sum(picked * keep[...].astype(F32), axis=1, keepdims=True)
    lane = lax.broadcasted_iota(jnp.int32, (1152, 128), 1)
    hit = (lane.astype(F32) == name) | (lane == 8)
    classes[...] = jnp.where(hit, 1.0, 0.0).astype(BF)
    copy.wait()


def rim_kernel(left_all, right_all, classes, down, up):
    left, right = left_all[:144].astype(F32), right_all[:144].astype(F32)
    marks = classes[864:].astype(F32)
    up[...] = jnp.concatenate([right[:72], left[:72]], axis=0).astype(BF)
    wide = jnp.concatenate([marks[b * 72:b * 72 + 72] for b in range(4)], axis=1)
    down[...] = jnp.concatenate([right[72:], left[72:], wide], axis=0).astype(BF)


def windows_of(right, left):
    parts = []
    for at in range(0, right.shape[0], 72):
        parts += [right[at:at + 72], left[at:at + 72]]
    return jnp.concatenate(parts, axis=0)


def halves_of(rows):
    right = [rows[at:at + 72] for at in range(0, rows.shape[0], 144)]
    left = [rows[at + 72:at + 144] for at in range(0, rows.shape[0], 144)]
    return jnp.concatenate(right, axis=0).astype(BF), jnp.concatenate(left, axis=0).astype(BF)


def project(x, w3, ones, srow, first=None):
    q = unit(dot_nt(x[:first], w3[0]).astype(BF), ones[...], srow[...])
    k = unit(dot_nt(x, w3[1]).astype(BF), ones[...])
    return q, k, dot_nt(x, w3[2]).astype(BF)


def first_kernel(right, left, classes, w3, out, ones, lanes, srow, hr, hl):
    wide = windows_of(right[144:432].astype(F32), left[144:432].astype(F32))
    q, k, v = project(wide.astype(BF), w3, ones, srow)
    att = []
    for at in range(0, 576, 144):
        span = slice(at, at + 144)
        mark = classes[span]
        att.append(heads(q[span], k[span], v[span], lanes[...], mark * lanes[2:3], mark))
    hr[...], hl[...] = halves_of(wide + normed(dot(jnp.concatenate(att, axis=0), out[...])))


def second_kernel(right_all, left_all, down, up, classes, w3, out, ones, lanes, srow, hr, hl):
    right, left = (
        jnp.concatenate([ref[432:].astype(F32), ref[:144].astype(F32)], axis=0)
        for ref in (right_all, left_all)
    )
    wide = windows_of(right, left)
    x = jnp.concatenate([wide.astype(BF), down[:144], up[...]], axis=0)
    q, k, v = project(x, w3, ones, srow, 576)
    got = down[144:216]
    far = jnp.concatenate([got[:, b * 128:b * 128 + 128].astype(F32) for b in range(4)], axis=0)
    far = far.astype(BF)
    att = []
    for at in (0, 144):
        span = slice(at, at + 144)
        mark = classes[576 + at:720 + at]
        att.append(heads(q[span], k[span], v[span], lanes[...], mark * lanes[2:3], mark))
    marks = (jnp.concatenate([far[144:], far[:144]], axis=0), classes[864:1152])
    for e in range(2):
        own, ext = slice(288 + e * 144, 432 + e * 144), slice(576 + e * 144, 720 + e * 144)
        keys = jnp.concatenate([k[own], k[ext]], axis=0)
        values = jnp.concatenate([v[own], v[ext]], axis=0)
        att.append(
            heads(q[own], keys, values, lanes[...], marks[e][:144] * lanes[2:3], marks[e])
        )
    hr[...], hl[...] = halves_of(wide + normed(dot(jnp.concatenate(att, axis=0), out[...])))


def feed_one(h, expand, shrink):
    grown = gelu(dot(h, expand[...])).astype(BF)
    return (h.astype(F32) + normed(dot(grown, shrink[...]))).astype(BF)


def feed_kernel(h1, h2, expand, shrink, out1, out2):
    out1[...] = feed_one(h1[...], expand, shrink)
    out2[...] = feed_one(h2[...], expand, shrink)


def feed_some_kernel(h, expand, shrink, out):
    out[...] = feed_one(h[...], expand, shrink)


def merge_kernel(l1, l2, r1, r2, pm, weight, coarse, ball, *, g):
    for half, (one, two) in enumerate(((l1, l2), (r1, r2))):
        for n, block in enumerate((two[144:], (one[:144], one[144:])[g], (one[144:], two[:144])[g])):
            ball[288 * n + half * 144:288 * n + half * 144 + 144] = block
    picked = dot(pm[g], ball[...])
    quartet = jnp.concatenate([picked[m * 144:m * 144 + 144] for m in range(4)], axis=1)
    coarse[...] = dot(normed(quartet).astype(BF), weight[...]).astype(BF)


def skip_kernel(l1, l2, r1, r2, perm, skip):
    for half, (one, two) in enumerate(((l1, l2), (r1, r2))):
        own = jnp.concatenate([two[144:], one[...], two[:144]], axis=0)
        got = dot(perm[...], own).astype(BF)
        for l in range(4):
            at = l * 288 + half * 144
            skip[at:at + 144] = got[l * 144:l * 144 + 144]


def attend_two_kernel(me, own, other, w3, ones, lanes, srow, x_out, att_out):
    a, b = own[...].astype(F32), other[...].astype(F32)
    first = me[0] == 0
    t0, t1 = jnp.where(first, a, b), jnp.where(first, b, a)
    x = jnp.concatenate([t0[:72], t1[:72], t0[72:], t1[72:]], axis=0).astype(BF)
    x_out[...] = x
    q = unit(dot_nt(x, w3[0]).astype(BF), ones[...], srow[...])
    k = unit(dot_nt(x, w3[1]).astype(BF), ones[...])
    v = dot_nt(x, w3[2]).astype(BF)
    for lg in range(2):
        span = slice(lg * 144, lg * 144 + 144)
        att_out[span] = heads(q[span], k[span], v[span], lanes[...])


def feed_two_kernel(
    me, quad, x, mine, theirs, o_mine, oa, ob, oc, od, expand, shrink, keep, send, hid_own, o_theirs
):
    for step, part in enumerate((oa, ob, oc, od)):
        at = pl.multiple_of((quad[0] ^ step) * 128, 128)
        o_theirs[pl.ds(at, 128)] = part[...]
    branch = dot(mine[...], o_mine[...]) + dot(theirs[...], o_theirs[...])
    hid = (x[...].astype(F32) + normed(branch)).astype(BF)
    acc = dot(gelu(dot_nt(hid, expand[...])).astype(BF), shrink[...])
    first = me[0] == 0

    def split(values):
        p0 = jnp.concatenate([values[0:72], values[144:216]], axis=0)
        p1 = jnp.concatenate([values[72:144], values[216:288]], axis=0)
        return jnp.where(first, p0, p1), jnp.where(first, p1, p0)

    own, far = split(acc)
    keep[...] = own
    send[...] = far.astype(BF)
    hid_own[...] = split(hid.astype(F32))[0].astype(BF)


def finish_rows(k, r, h, pout):
    done = (h[...].astype(F32) + normed(k[...] + r[...].astype(F32))).astype(BF)
    return dot(pout[...], done).reshape(6, 6, 4, 1024).astype(BF)


def finish_first_kernel(k, r, h, pout, rows):
    rows[...] = finish_rows(k, r, h, pout)


def finish_kernel(first, k, r, h, pout, coarse):
    coarse[:6] = first[...]
    coarse[6:] = finish_rows(k, r, h, pout)


def behind(value, axis, steps):
    count = lax.axis_size(axis)
    return lax.ppermute(value, axis, [(s, (s + steps) % count) for s in range(count)])


def after(value, done):
    return lax.optimization_barrier((value, done))[0]


def across(value, axis, flip):
    return lax.ppermute(value, axis, [(s, s ^ flip) for s in range(lax.axis_size(axis))])


def shards(
    patches,
    region_ids,
    triple_one,
    output_one,
    expand_one,
    shrink_one,
    scales_one,
    merge_weight,
    triple_two,
    output_two,
    expand_two,
    shrink_two,
    scales_two,
):
    me = lax.axis_index("tp").astype(jnp.int32).reshape(1)
    quad = (lax.axis_index("lat") & 3).astype(jnp.int32).reshape(1)
    ones = const(np.kron(np.eye(4), np.ones((64, 64))))
    lane_of = np.zeros((8, 128), np.float32)
    lane_of[0, :64] = 1
    lane_of[1, 64:] = 1
    lane_of[2] = MASK
    lane_of[2, 8] = -MASK
    lanes = const(lane_of)
    spread = const(np.kron(np.eye(8), np.ones((1, 64))))
    col_axes = ("lon", "tp")
    tok = lambda n: ((n, 512), BF)

    home = patches.transpose(0, 2, 1, 3).reshape(4, 2, 144, 512)
    left = call(pack_kernel, [tok(576)], [home[:, 0]], 10**8)[0]
    right = call(pack_kernel, [tok(576)], [after(home, left)[:, 1]], 10**9)[0]
    region_ids = after(region_ids, right)
    left = behind(left, col_axes, -1)
    pick, keep = pick_rows()
    classes, s_one, s_two, part = call(
        ready_kernel,
        [((1152, 128), BF), ((1, 512), F32), ((1, 512), F32), ((128, 1024), BF)],
        [
            quad,
            region_ids.transpose(2, 0, 1),
            const(pick),
            const(keep),
            scales_one.reshape(1, 8),
            scales_two.reshape(1, 8),
            spread,
            output_two,
        ],
        10**9,
        smem=(0,),
        hbm=(7,),
        scratch=[pltpu.SemaphoreType.DMA],
    )
    oa = behind(after(part, left), "tp", 1)
    down, up = call(rim_kernel, [tok(216), tok(144)], [left, right, classes], 10**6)
    classes = after(classes, down)
    down, up = behind(down, "lat", 1), behind(up, "lat", -1)

    w_one = triple_one.transpose(1, 0, 2)
    shared = [classes, w_one, output_one, ones, lanes, s_one]
    hr1, hl1 = call(first_kernel, [tok(288)] * 2, [right, left] + shared, 4 * 10**9)
    hl1 = behind(hl1, col_axes, 1)
    shared[0] = after(classes, hr1)
    hr2, hl2 = call(
        second_kernel, [tok(288)] * 2, [right, left, down, up] + shared, 15 * 10**8
    )
    hl2 = behind(hl2, col_axes, 1)

    feeds = [expand_one, shrink_one]
    br1, br2 = call(feed_kernel, [tok(288)] * 2, [hr1, hr2] + feeds, 3 * 10**9)
    bl1 = call(feed_some_kernel, [tok(288)], [after(hl1, (br1, oa))] + feeds, 2 * 10**9)[0]
    oa = after(oa, bl1)
    ob, oc = across(oa, "lat", 1), across(oa, "lat", 2)
    bl2 = call(feed_some_kernel, [tok(288)], [after(hl2, bl1)] + feeds, 2 * 10**9)[0]
    blocks = [bl1, bl2, br1, br2]
    pm, coarse_in = const(merge_rows()), []
    for g in range(2):
        if g:
            blocks = [after(blocks[0], coarse_in[0])] + blocks[1:]
        coarse_in += call(
            functools.partial(merge_kernel, g=g),
            [((144, 1024), BF)],
            blocks + [pm, merge_weight],
            10**9,
            scratch=[pltpu.VMEM((864, 512), BF)],
        )
    c0, c1 = coarse_in
    d0, d1 = behind(c0, "tp", 1), behind(c1, "tp", 1)
    od = across(after(oc, (c1, ob)), "lat", 1)
    blocks[0] = after(blocks[0], c1)
    skip = call(skip_kernel, [tok(1152)], blocks + [const(home_rows())], 2 * 10**9)[0]
    c0, skip = lax.optimization_barrier((c0, skip))
    skip = skip.reshape(4, 12, 24, 512).transpose(0, 2, 1, 3)
    w_two = triple_two.transpose(1, 0, 2)
    attended = []
    for own, other in ((c0, d0), (c1, d1)):
        if attended:
            own = after(own, (attended[0][1], od))
        x, mine = call(
            attend_two_kernel,
            [((288, 1024), BF), tok(288)],
            [me, own, other, w_two, ones, lanes, s_two],
            2 * 10**9,
            smem=(0,),
        )
        attended.append((x, mine, behind(mine, "tp", 1)))
    kept = []
    for x, mine, theirs in attended:
        if kept:
            x = after(x, kept[0][0])
        keep, send, hid_own = call(
            feed_two_kernel,
            [((144, 1024), F32), ((144, 1024), BF), ((144, 1024), BF)],
            [me, quad, x, mine, theirs, output_two, oa, ob, oc, od, expand_two, shrink_two],
            10**8,
            smem=(0, 1),
            scratch=[pltpu.VMEM((512, 1024), BF)],
        )
        kept.append((keep, behind(send, "tp", 1), hid_own))
    pout = const(coarse_rows())
    first = call(finish_first_kernel, [((6, 6, 4, 1024), BF)], [*kept[0], pout], 10**8)[0]
    coarse = call(finish_kernel, [((12, 6, 4, 1024), BF)], [first, *kept[1], pout], 10**8)[0]
    return (skip, coarse.transpose(2, 0, 1, 3))


def solution(mesh):
    in_specs = (
        P(None, "lat", ("lon", "tp"), None),
        P(None, "lat", ("lon", "tp")),
        P(),
        P(),
        P(),
        P(),
        P(),
        P(),
        P("tp", None, None),
        P("tp", None),
        P("tp", None),
        P("tp", None),
        P("tp"),
    )
    out_specs = (P(None, "lat", ("lon", "tp"), None), P(None, "lat", ("lon", "tp"), None))
    return jax.shard_map(shards, mesh=mesh, in_specs=in_specs, out_specs=out_specs, check_vma=False)
```

```python
import functools
import math

import jax
import jax.numpy as jnp
import numpy as np
from jax import lax
from jax.experimental import pallas as pl
from jax.experimental.pallas import tpu as pltpu
from jax.sharding import PartitionSpec as P

BF = jnp.bfloat16
F32 = jnp.float32
MASK = 192.0
LOG2E = math.log2(math.e)
MIB = 1024 * 1024


def home_level(lg, l):
    return (2 * lg + l + 1) % 4


def pick_rows():
    rows, keep = np.zeros((1152, 48), np.float32), np.zeros((1152, 24), np.float32)
    group = np.zeros((1152, 1), np.float32)
    at = 0
    for w in range(4):
        for part in range(2 if w == 3 else 1):
            outer = [(h, g) for h in range(2) for g in range(2)]
            if w < 3:
                outer = [(h, g) for g in range(2) for h in range(2)]
            for half, lg in outer:
                for l in range(2):
                    for i in range(3 * part, 3 * part + 3) if w == 3 else range(6):
                        for j in range(6):
                            rows[at, (half * 6 + j) * 4 + 2 * lg + l] = 1
                            keep[at, 6 * w + i] = 1
                            group[at] = 4 * lg
                            at += 1
    return rows, np.concatenate([keep, group], axis=1)


def place(level, i, j):
    lg, l = ((level - 1) % 4) // 2, ((level - 1) % 4) % 2
    if i < 3 or i >= 21:
        edge, ie = (0, i) if i < 3 else (1, i - 21)
        return edge * 72 + lg * 36 + l * 18 + ie * 6 + j
    w, iw = (i - 3) // 6, (i - 3) % 6
    return 144 + w * 144 + lg * 72 + l * 36 + iw * 6 + j


def home_rows():
    mat = np.zeros((576, 576), np.float32)
    for level in range(4):
        for j in range(6):
            for i in range(24):
                mat[level * 144 + j * 24 + i, place(level, i, j)] = 1
    return mat


def merge_rows():
    mat = np.zeros((2, 4, 144, 864), np.float32)
    for g in range(2):
        for m in range(4):
            pi, pj = m // 2, m % 2
            for level in range(4):
                for ii in range(6):
                    i = 2 * (6 * g + ii) + pi
                    for jj in range(6):
                        half, j = jj // 3, 2 * (jj % 3) + pj
                        at = place(level, i, j)
                        chunk = 0 if at < 144 else at // 144 - g
                        row = (level // 2) * 72 + (level % 2) * 36 + ii * 6 + jj
                        mat[g, m, row, 288 * chunk + half * 144 + at % 144] = 1
    return mat.reshape(2, 576, 864)


def coarse_rows():
    mat = np.zeros((144, 144), np.float32)
    for level in range(4):
        for ii in range(6):
            for jj in range(6):
                row = (ii * 6 + jj) * 4 + level
                mat[row, (level // 2) * 72 + (level % 2) * 36 + ii * 6 + jj] = 1
    return mat


def const(mat):
    return jnp.asarray(mat, dtype=BF)


def dot(a, b):
    return lax.dot_general(a, b, (((1,), (0,)), ((), ())), preferred_element_type=F32)


def dot_nt(a, b):
    return lax.dot_general(a, b, (((1,), (1,)), ((), ())), preferred_element_type=F32)


def normed(values):
    centred = values - jnp.mean(values, axis=-1, keepdims=True)
    spread = jnp.mean(centred * centred, axis=-1, keepdims=True)
    return centred * lax.rsqrt(spread + 1e-05)


def gelu(x):
    inner = x * (0.7978845608028654 + 0.035677408136300125 * (x * x))
    return (0.5 * x) * (1.0 + jnp.tanh(inner))


def unit(packed, ones, factor=None):
    wide = packed.astype(F32)
    squares = (wide * wide).astype(BF)
    total = jnp.concatenate([dot(squares[:, :256], ones), dot(squares[:, 256:], ones)], axis=1)
    result = wide * lax.rsqrt(total + 1e-06)
    if factor is not None:
        result = result * factor
    return result.astype(BF)


def heads(q, k, v, lanes, aug_q=None, aug_k=None):
    count = q.shape[0]
    low, high = lanes[0:1], lanes[1:2]
    first = lax.broadcasted_iota(jnp.int32, (count, 128), 1) < 64
    if aug_q is not None:
        aug_q = jnp.concatenate([aug_q, aug_q], axis=0)
    ones = jnp.ones((v.shape[0], 128), BF)
    parts = []
    for pair in range(4):
        span = slice(pair * 128, pair * 128 + 128)
        qp, kp = q[:, span], k[:, span]
        qp = jnp.concatenate([qp * low, qp * high], axis=0)
        if aug_q is not None:
            qp = jnp.concatenate([qp, aug_q], axis=1)
            kp = jnp.concatenate([kp, aug_k], axis=1)
        weights = jnp.exp2(dot_nt(qp, kp)).astype(BF)
        acc = dot(weights, jnp.concatenate([v[:, span], ones], axis=1))
        both = jnp.where(first, acc[:count, :128], acc[count:, :128])
        total = jnp.where(first, acc[:count, 128:], acc[count:, 128:])
        parts.append(both / total)
    return jnp.concatenate(parts, axis=1).astype(BF)


def call(kernel, outs, args, flops, vmem=16, smem=(), hbm=(), scratch=()):
    def space(n):
        return pltpu.SMEM if n in smem else pltpu.HBM if n in hbm else pltpu.VMEM

    moved = sum(int(np.prod(a.shape)) * a.dtype.itemsize for a in args)
    return pl.pallas_call(
        kernel,
        out_shape=[jax.ShapeDtypeStruct(shape, kind) for shape, kind in outs],
        in_specs=[pl.BlockSpec(memory_space=space(n)) for n in range(len(args))],
        out_specs=[pl.BlockSpec(memory_space=pltpu.VMEM) for _ in outs],
        scratch_shapes=list(scratch),
        compiler_params=pltpu.CompilerParams(vmem_limit_bytes=vmem * MIB),
        cost_estimate=pl.CostEstimate(flops=flops, bytes_accessed=moved, transcendentals=0),
    )(*args)


def pack_kernel(x, left, right):
    row = lax.broadcasted_iota(jnp.int32, (144, 144), 0)
    col = lax.broadcasted_iota(jnp.int32, (144, 144), 1)
    six = (row * 10923) >> 16
    lat = jnp.where(row < 18, six, jnp.where(row < 36, six + 18, six - 3))
    perm = jnp.where(col == (row - 6 * six) * 24 + lat, 1.0, 0.0).astype(BF)
    for half, dst in enumerate((left, right)):
        got = []
        for level in (1, 2, 3, 0):
            at = level * 288 + half * 144
            got.append(dot(perm, x[at:at + 144]))
        rows = [g[e:e + 18] for e in (0, 18) for g in got]
        dst[:144] = jnp.concatenate(rows, axis=0).astype(BF)
        rows = [g[w:w + 36] for w in (36, 72, 108) for g in got]
        dst[144:] = jnp.concatenate(rows, axis=0).astype(BF)


def ready_kernel(
    at, ids, rows, keep, sone, stwo, spread, o_two, classes, s_one, s_two, quarter, sem
):
    copy = pltpu.make_async_copy(
        o_two.at[pl.ds(pl.multiple_of(at[0] * 128, 128), 128)], quarter, sem
    )
    copy.start()
    for src, dst in ((sone, s_one), (stwo, s_two)):
        dst[...] = dot(src[...], spread[...])[0:1] * LOG2E
    grid = jnp.concatenate([ids[c] for c in range(12)], axis=0).astype(F32).astype(BF)
    picked = jnp.concatenate([dot(rows[...], grid), jnp.ones((1152, 1), F32)], axis=1)
    name = jnp.sum(picked * keep[...].astype(F32), axis=1, keepdims=True)
    lane = lax.broadcasted_iota(jnp.int32, (1152, 128), 1)
    hit = (lane.astype(F32) == name) | (lane == 8)
    classes[...] = jnp.where(hit, 1.0, 0.0).astype(BF)
    copy.wait()


def rim_kernel(left_all, right_all, classes, down, up):
    left, right = left_all[:144].astype(F32), right_all[:144].astype(F32)
    marks = classes[864:].astype(F32)
    up[...] = jnp.concatenate([right[:72], left[:72]], axis=0).astype(BF)
    wide = jnp.concatenate([marks[b * 72:b * 72 + 72] for b in range(4)], axis=1)
    down[...] = jnp.concatenate([right[72:], left[72:], wide], axis=0).astype(BF)


def join_kernel(at, a, b, c, d, out):
    mine = at[0]
    for step, part in enumerate((a, b, c, d)):
        out[pl.ds(pl.multiple_of((mine ^ step) * 128, 128), 128)] = part[...]


def windows_of(right, left):
    parts = []
    for at in range(0, right.shape[0], 72):
        parts += [right[at:at + 72], left[at:at + 72]]
    return jnp.concatenate(parts, axis=0)


def halves_of(rows):
    right = [rows[at:at + 72] for at in range(0, rows.shape[0], 144)]
    left = [rows[at + 72:at + 144] for at in range(0, rows.shape[0], 144)]
    return jnp.concatenate(right, axis=0).astype(BF), jnp.concatenate(left, axis=0).astype(BF)


def project(x, w3, ones, srow, first=None):
    q = unit(dot_nt(x[:first], w3[0]).astype(BF), ones[...], srow[...])
    k = unit(dot_nt(x, w3[1]).astype(BF), ones[...])
    return q, k, dot_nt(x, w3[2]).astype(BF)


def first_kernel(right, left, classes, w3, out, ones, lanes, srow, hr, hl):
    wide = windows_of(right[144:432].astype(F32), left[144:432].astype(F32))
    q, k, v = project(wide.astype(BF), w3, ones, srow)
    att = []
    for at in range(0, 576, 144):
        span = slice(at, at + 144)
        mark = classes[span]
        att.append(heads(q[span], k[span], v[span], lanes[...], mark * lanes[2:3], mark))
    hr[...], hl[...] = halves_of(wide + normed(dot(jnp.concatenate(att, axis=0), out[...])))


def second_kernel(right_all, left_all, down, up, classes, w3, out, ones, lanes, srow, hr, hl):
    right, left = (
        jnp.concatenate([ref[432:].astype(F32), ref[:144].astype(F32)], axis=0)
        for ref in (right_all, left_all)
    )
    wide = windows_of(right, left)
    x = jnp.concatenate([wide.astype(BF), down[:144], up[...]], axis=0)
    q, k, v = project(x, w3, ones, srow, 576)
    got = down[144:216]
    far = jnp.concatenate([got[:, b * 128:b * 128 + 128].astype(F32) for b in range(4)], axis=0)
    far = far.astype(BF)
    att = []
    for at in (0, 144):
        span = slice(at, at + 144)
        mark = classes[576 + at:720 + at]
        att.append(heads(q[span], k[span], v[span], lanes[...], mark * lanes[2:3], mark))
    marks = (jnp.concatenate([far[144:], far[:144]], axis=0), classes[864:1152])
    for e in range(2):
        own, ext = slice(288 + e * 144, 432 + e * 144), slice(576 + e * 144, 720 + e * 144)
        keys = jnp.concatenate([k[own], k[ext]], axis=0)
        values = jnp.concatenate([v[own], v[ext]], axis=0)
        att.append(
            heads(q[own], keys, values, lanes[...], marks[e][:144] * lanes[2:3], marks[e])
        )
    hr[...], hl[...] = halves_of(wide + normed(dot(jnp.concatenate(att, axis=0), out[...])))


def feed_one(h, expand, shrink):
    grown = gelu(dot(h, expand[...])).astype(BF)
    return (h.astype(F32) + normed(dot(grown, shrink[...]))).astype(BF)


def feed_kernel(h1, h2, expand, shrink, out1, out2):
    out1[...] = feed_one(h1[...], expand, shrink)
    out2[...] = feed_one(h2[...], expand, shrink)


def feed_some_kernel(h, expand, shrink, out):
    out[...] = feed_one(h[...], expand, shrink)


def merge_kernel(l1, l2, r1, r2, pm, weight, coarse, ball, *, g):
    for half, (one, two) in enumerate(((l1, l2), (r1, r2))):
        for n, block in enumerate((two[144:], (one[:144], one[144:])[g], (one[144:], two[:144])[g])):
            ball[288 * n + half * 144:288 * n + half * 144 + 144] = block
    picked = dot(pm[g], ball[...])
    quartet = jnp.concatenate([picked[m * 144:m * 144 + 144] for m in range(4)], axis=1)
    coarse[...] = dot(normed(quartet).astype(BF), weight[...]).astype(BF)


def skip_kernel(l1, l2, r1, r2, perm, skip):
    for half, (one, two) in enumerate(((l1, l2), (r1, r2))):
        own = jnp.concatenate([two[144:], one[...], two[:144]], axis=0)
        got = dot(perm[...], own).astype(BF)
        for l in range(4):
            at = l * 288 + half * 144
            skip[at:at + 144] = got[l * 144:l * 144 + 144]


def attend_two_kernel(me, own, other, w3, ones, lanes, srow, x_out, att_out):
    a, b = own[...].astype(F32), other[...].astype(F32)
    first = me[0] == 0
    t0, t1 = jnp.where(first, a, b), jnp.where(first, b, a)
    x = jnp.concatenate([t0[:72], t1[:72], t0[72:], t1[72:]], axis=0).astype(BF)
    x_out[...] = x
    q = unit(dot_nt(x, w3[0]).astype(BF), ones[...], srow[...])
    k = unit(dot_nt(x, w3[1]).astype(BF), ones[...])
    v = dot_nt(x, w3[2]).astype(BF)
    for lg in range(2):
        span = slice(lg * 144, lg * 144 + 144)
        att_out[span] = heads(q[span], k[span], v[span], lanes[...])


def feed_two_kernel(me, x, mine, theirs, o_mine, o_theirs, expand, shrink, keep, send, hid_own):
    branch = dot(mine[...], o_mine[...]) + dot(theirs[...], o_theirs[...])
    hid = (x[...].astype(F32) + normed(branch)).astype(BF)
    acc = dot(gelu(dot_nt(hid, expand[...])).astype(BF), shrink[...])
    first = me[0] == 0

    def split(values):
        p0 = jnp.concatenate([values[0:72], values[144:216]], axis=0)
        p1 = jnp.concatenate([values[72:144], values[216:288]], axis=0)
        return jnp.where(first, p0, p1), jnp.where(first, p1, p0)

    own, far = split(acc)
    keep[...] = own
    send[...] = far.astype(BF)
    hid_own[...] = split(hid.astype(F32))[0].astype(BF)


def finish_rows(k, r, h, pout):
    done = (h[...].astype(F32) + normed(k[...] + r[...].astype(F32))).astype(BF)
    return dot(pout[...], done).reshape(6, 6, 4, 1024).astype(BF)


def finish_first_kernel(k, r, h, pout, rows):
    rows[...] = finish_rows(k, r, h, pout)


def finish_kernel(first, k, r, h, pout, coarse):
    coarse[:6] = first[...]
    coarse[6:] = finish_rows(k, r, h, pout)


def behind(value, axis, steps):
    count = lax.axis_size(axis)
    return lax.ppermute(value, axis, [(s, (s + steps) % count) for s in range(count)])


def after(value, done):
    return lax.optimization_barrier((value, done))[0]


def across(value, axis, flip):
    return lax.ppermute(value, axis, [(s, s ^ flip) for s in range(lax.axis_size(axis))])


def shards(
    patches,
    region_ids,
    triple_one,
    output_one,
    expand_one,
    shrink_one,
    scales_one,
    merge_weight,
    triple_two,
    output_two,
    expand_two,
    shrink_two,
    scales_two,
):
    me = lax.axis_index("tp").astype(jnp.int32).reshape(1)
    lat_at = (lax.axis_index("lat") & 3).astype(jnp.int32).reshape(1)
    ones = const(np.kron(np.eye(4), np.ones((64, 64))))
    lane_of = np.zeros((8, 128), np.float32)
    lane_of[0, :64] = 1
    lane_of[1, 64:] = 1
    lane_of[2] = MASK
    lane_of[2, 8] = -MASK
    lanes = const(lane_of)
    spread = const(np.kron(np.eye(8), np.ones((1, 64))))
    col_axes = ("lon", "tp")
    tok = lambda n: ((n, 512), BF)

    flat = patches.transpose(0, 2, 1, 3).reshape(1152, 512)
    left, right = call(
        pack_kernel,
        [tok(576)] * 2,
        [flat],
        10**9,
    )
    region_ids = after(region_ids, right)
    left = behind(left, col_axes, -1)
    pick, keep = pick_rows()
    classes, s_one, s_two, quarter = call(
        ready_kernel,
        [((1152, 128), BF), ((1, 512), F32), ((1, 512), F32), ((128, 1024), BF)],
        [
            lat_at,
            region_ids.transpose(2, 0, 1),
            const(pick),
            const(keep),
            scales_one.reshape(1, 8),
            scales_two.reshape(1, 8),
            spread,
            output_two,
        ],
        10**9,
        smem=(0,),
        hbm=(7,),
        scratch=[pltpu.SemaphoreType.DMA],
    )
    quarter = after(quarter, left)
    oa = behind(quarter, "tp", 1)
    down, up = call(rim_kernel, [tok(216), tok(144)], [left, right, classes], 10**6)
    classes = after(classes, down)
    down, up = behind(down, "lat", 1), behind(up, "lat", -1)

    w_one = triple_one.transpose(1, 0, 2)
    shared = [classes, w_one, output_one, ones, lanes, s_one]
    hr1, hl1 = call(first_kernel, [tok(288)] * 2, [right, left] + shared, 4 * 10**9)
    hl1 = behind(hl1, col_axes, 1)
    shared[0] = after(classes, hr1)
    hr2, hl2 = call(
        second_kernel, [tok(288)] * 2, [right, left, down, up] + shared, 6 * 10**9
    )
    hl2 = behind(hl2, col_axes, 1)

    feeds = [expand_one, shrink_one]
    br1, br2 = call(feed_kernel, [tok(288)] * 2, [hr1, hr2] + feeds, 3 * 10**9)
    bl1 = call(feed_some_kernel, [tok(288)], [after(hl1, br1)] + feeds, 2 * 10**9)[0]
    oa = after(oa, bl1)
    ob, oc = across(oa, "lat", 1), across(oa, "lat", 2)
    bl2 = call(feed_some_kernel, [tok(288)], [after(hl2, bl1)] + feeds, 2 * 10**9)[0]
    blocks = [bl1, bl2, br1, br2]
    od = across(after(oc, bl2), "lat", 1)
    pm, coarse_in = const(merge_rows()), []
    for g in range(2):
        if g:
            blocks = [after(blocks[0], coarse_in[0])] + blocks[1:]
        coarse_in += call(
            functools.partial(merge_kernel, g=g),
            [((144, 1024), BF)],
            blocks + [pm, merge_weight],
            10**9,
            scratch=[pltpu.VMEM((864, 512), BF)],
        )
    c0, c1 = coarse_in
    d0, d1 = behind(c0, "tp", 1), behind(c1, "tp", 1)
    blocks[0], od = after(blocks[0], c1), after(od, c1)
    skip = call(skip_kernel, [tok(1152)], blocks + [const(home_rows())], 2 * 10**9)[0]
    o_theirs = call(
        join_kernel, [((512, 1024), BF)], [lat_at, oa, ob, oc, od], 10**9, smem=(0,)
    )[0]
    c0, skip, o_theirs = lax.optimization_barrier((c0, skip, o_theirs))
    skip = skip.reshape(4, 12, 24, 512).transpose(0, 2, 1, 3)

    w_two = triple_two.transpose(1, 0, 2)
    attended = []
    for own, other in ((c0, d0), (c1, d1)):
        if attended:
            own = after(own, attended[0][1])
        x, mine = call(
            attend_two_kernel,
            [((288, 1024), BF), tok(288)],
            [me, own, other, w_two, ones, lanes, s_two],
            2 * 10**9,
            smem=(0,),
        )
        attended.append((x, mine, behind(mine, "tp", 1)))
    kept = []
    for x, mine, theirs in attended:
        if kept:
            x = after(x, kept[0][0])
        keep, send, hid_own = call(
            feed_two_kernel,
            [((144, 1024), F32), ((144, 1024), BF), ((144, 1024), BF)],
            [me, x, mine, theirs, output_two, o_theirs, expand_two, shrink_two],
            10**8,
            smem=(0,),
        )
        kept.append((keep, behind(send, "tp", 1), hid_own))
    pout = const(coarse_rows())
    first = call(finish_first_kernel, [((6, 6, 4, 1024), BF)], [*kept[0], pout], 10**8)[0]
    coarse = call(finish_kernel, [((12, 6, 4, 1024), BF)], [first, *kept[1], pout], 10**8)[0]
    return (skip, coarse.transpose(2, 0, 1, 3))


def solution(mesh):
    in_specs = (
        P(None, "lat", ("lon", "tp"), None),
        P(None, "lat", ("lon", "tp")),
        P(),
        P(),
        P(),
        P(),
        P(),
        P(),
        P("tp", None, None),
        P("tp", None),
        P("tp", None),
        P("tp", None),
        P("tp"),
    )
    out_specs = (P(None, "lat", ("lon", "tp"), None), P(None, "lat", ("lon", "tp"), None))
    return jax.shard_map(shards, mesh=mesh, in_specs=in_specs, out_specs=out_specs, check_vma=False)
```

```python
import functools
import math

import jax
import jax.numpy as jnp
import numpy as np
from jax import lax
from jax.experimental import pallas as pl
from jax.experimental.pallas import tpu as pltpu
from jax.sharding import PartitionSpec as P

BF = jnp.bfloat16
F32 = jnp.float32
MASK = 192.0
LOG2E = math.log2(math.e)
MIB = 1024 * 1024


def home_level(lg, l):
    return (2 * lg + l + 1) % 4


def pick_rows():
    rows, keep = np.zeros((1152, 48), np.float32), np.zeros((1152, 24), np.float32)
    group = np.zeros((1152, 1), np.float32)
    at = 0
    for w in range(4):
        for part in range(2 if w == 3 else 1):
            outer = [(h, g) for h in range(2) for g in range(2)]
            if w < 3:
                outer = [(h, g) for g in range(2) for h in range(2)]
            for half, lg in outer:
                for l in range(2):
                    for i in range(3 * part, 3 * part + 3) if w == 3 else range(6):
                        for j in range(6):
                            rows[at, (half * 6 + j) * 4 + 2 * lg + l] = 1
                            keep[at, 6 * w + i] = 1
                            group[at] = 4 * lg
                            at += 1
    return rows, np.concatenate([keep, group], axis=1)


def place(level, i, j):
    lg, l = ((level - 1) % 4) // 2, ((level - 1) % 4) % 2
    if i < 3 or i >= 21:
        edge, ie = (0, i) if i < 3 else (1, i - 21)
        return edge * 72 + lg * 36 + l * 18 + ie * 6 + j
    w, iw = (i - 3) // 6, (i - 3) % 6
    return 144 + w * 144 + lg * 72 + l * 36 + iw * 6 + j


def home_rows():
    mat = np.zeros((576, 576), np.float32)
    for level in range(4):
        for j in range(6):
            for i in range(24):
                mat[level * 144 + j * 24 + i, place(level, i, j)] = 1
    return mat


def merge_rows():
    mat = np.zeros((2, 4, 144, 864), np.float32)
    for g in range(2):
        for m in range(4):
            pi, pj = m // 2, m % 2
            for level in range(4):
                for ii in range(6):
                    i = 2 * (6 * g + ii) + pi
                    for jj in range(6):
                        half, j = jj // 3, 2 * (jj % 3) + pj
                        at = place(level, i, j)
                        chunk = 0 if at < 144 else at // 144 - g
                        row = (level // 2) * 72 + (level % 2) * 36 + ii * 6 + jj
                        mat[g, m, row, 288 * chunk + half * 144 + at % 144] = 1
    return mat.reshape(2, 576, 864)


def coarse_rows():
    mat = np.zeros((144, 144), np.float32)
    for level in range(4):
        for ii in range(6):
            for jj in range(6):
                row = (ii * 6 + jj) * 4 + level
                mat[row, (level // 2) * 72 + (level % 2) * 36 + ii * 6 + jj] = 1
    return mat


def const(mat):
    return jnp.asarray(mat, dtype=BF)


def dot(a, b):
    return lax.dot_general(a, b, (((1,), (0,)), ((), ())), preferred_element_type=F32)


def dot_nt(a, b):
    return lax.dot_general(a, b, (((1,), (1,)), ((), ())), preferred_element_type=F32)


def normed(values):
    centred = values - jnp.mean(values, axis=-1, keepdims=True)
    spread = jnp.mean(centred * centred, axis=-1, keepdims=True)
    return centred * lax.rsqrt(spread + 1e-05)


def gelu(x):
    inner = x * (0.7978845608028654 + 0.035677408136300125 * (x * x))
    return (0.5 * x) * (1.0 + jnp.tanh(inner))


def unit(packed, ones, factor=None):
    wide = packed.astype(F32)
    squares = (wide * wide).astype(BF)
    total = jnp.concatenate([dot(squares[:, :256], ones), dot(squares[:, 256:], ones)], axis=1)
    result = wide * lax.rsqrt(total + 1e-06)
    if factor is not None:
        result = result * factor
    return result.astype(BF)


def heads(q, k, v, lanes, aug_q=None, aug_k=None):
    count = q.shape[0]
    low, high = lanes[0:1], lanes[1:2]
    first = lax.broadcasted_iota(jnp.int32, (count, 128), 1) < 64
    if aug_q is not None:
        aug_q = jnp.concatenate([aug_q, aug_q], axis=0)
    ones = jnp.ones((v.shape[0], 128), BF)
    parts = []
    for pair in range(4):
        span = slice(pair * 128, pair * 128 + 128)
        qp, kp = q[:, span], k[:, span]
        qp = jnp.concatenate([qp * low, qp * high], axis=0)
        if aug_q is not None:
            qp = jnp.concatenate([qp, aug_q], axis=1)
            kp = jnp.concatenate([kp, aug_k], axis=1)
        weights = jnp.exp2(dot_nt(qp, kp)).astype(BF)
        acc = dot(weights, jnp.concatenate([v[:, span], ones], axis=1))
        both = jnp.where(first, acc[:count, :128], acc[count:, :128])
        total = jnp.where(first, acc[:count, 128:], acc[count:, 128:])
        parts.append(both / total)
    return jnp.concatenate(parts, axis=1).astype(BF)


def call(kernel, outs, args, flops, vmem=16, smem=(), hbm=(), scratch=()):
    def space(n):
        return pltpu.SMEM if n in smem else pltpu.HBM if n in hbm else pltpu.VMEM

    moved = sum(int(np.prod(a.shape)) * a.dtype.itemsize for a in args)
    return pl.pallas_call(
        kernel,
        out_shape=[jax.ShapeDtypeStruct(shape, kind) for shape, kind in outs],
        in_specs=[pl.BlockSpec(memory_space=space(n)) for n in range(len(args))],
        out_specs=[pl.BlockSpec(memory_space=pltpu.VMEM) for _ in outs],
        scratch_shapes=list(scratch),
        compiler_params=pltpu.CompilerParams(vmem_limit_bytes=vmem * MIB),
        cost_estimate=pl.CostEstimate(flops=flops, bytes_accessed=moved, transcendentals=0),
    )(*args)


def pack_kernel(x, left, right):
    row = lax.broadcasted_iota(jnp.int32, (144, 144), 0)
    col = lax.broadcasted_iota(jnp.int32, (144, 144), 1)
    six = (row * 10923) >> 16
    lat = jnp.where(row < 18, six, jnp.where(row < 36, six + 18, six - 3))
    perm = jnp.where(col == (row - 6 * six) * 24 + lat, 1.0, 0.0).astype(BF)
    for half, dst in enumerate((left, right)):
        got = []
        for level in (1, 2, 3, 0):
            at = level * 288 + half * 144
            got.append(dot(perm, x[at:at + 144]))
        rows = [g[e:e + 18] for e in (0, 18) for g in got]
        dst[:144] = jnp.concatenate(rows, axis=0).astype(BF)
        rows = [g[w:w + 36] for w in (36, 72, 108) for g in got]
        dst[144:] = jnp.concatenate(rows, axis=0).astype(BF)


def ready_kernel(
    at, ids, rows, keep, sone, stwo, spread, o_two, classes, s_one, s_two, quarter, sem
):
    copy = pltpu.make_async_copy(
        o_two.at[pl.ds(pl.multiple_of(at[0] * 128, 128), 128)], quarter, sem
    )
    copy.start()
    for src, dst in ((sone, s_one), (stwo, s_two)):
        dst[...] = dot(src[...], spread[...])[0:1] * LOG2E
    grid = jnp.concatenate([ids[c] for c in range(12)], axis=0).astype(F32).astype(BF)
    picked = jnp.concatenate([dot(rows[...], grid), jnp.ones((1152, 1), F32)], axis=1)
    name = jnp.sum(picked * keep[...].astype(F32), axis=1, keepdims=True)
    lane = lax.broadcasted_iota(jnp.int32, (1152, 128), 1)
    hit = (lane.astype(F32) == name) | (lane == 8)
    classes[...] = jnp.where(hit, 1.0, 0.0).astype(BF)
    copy.wait()


def rim_kernel(left_all, right_all, classes, down, up):
    left, right = left_all[:144].astype(F32), right_all[:144].astype(F32)
    marks = classes[864:].astype(F32)
    up[...] = jnp.concatenate([right[:72], left[:72]], axis=0).astype(BF)
    wide = jnp.concatenate([marks[b * 72:b * 72 + 72] for b in range(4)], axis=1)
    down[...] = jnp.concatenate([right[72:], left[72:], wide], axis=0).astype(BF)


def join_kernel(at, a, b, c, d, out):
    mine = at[0]
    for step, part in enumerate((a, b, c, d)):
        out[pl.ds(pl.multiple_of((mine ^ step) * 128, 128), 128)] = part[...]


def windows_of(right, left):
    parts = []
    for at in range(0, right.shape[0], 72):
        parts += [right[at:at + 72], left[at:at + 72]]
    return jnp.concatenate(parts, axis=0)


def halves_of(rows):
    right = [rows[at:at + 72] for at in range(0, rows.shape[0], 144)]
    left = [rows[at + 72:at + 144] for at in range(0, rows.shape[0], 144)]
    return jnp.concatenate(right, axis=0).astype(BF), jnp.concatenate(left, axis=0).astype(BF)


def project(x, w3, ones, srow, first=None):
    q = unit(dot_nt(x[:first], w3[0]).astype(BF), ones[...], srow[...])
    k = unit(dot_nt(x, w3[1]).astype(BF), ones[...])
    return q, k, dot_nt(x, w3[2]).astype(BF)


def first_kernel(right, left, classes, w3, out, ones, lanes, srow, hr, hl):
    wide = windows_of(right[144:432].astype(F32), left[144:432].astype(F32))
    q, k, v = project(wide.astype(BF), w3, ones, srow)
    att = []
    for at in range(0, 576, 144):
        span = slice(at, at + 144)
        mark = classes[span]
        att.append(heads(q[span], k[span], v[span], lanes[...], mark * lanes[2:3], mark))
    hr[...], hl[...] = halves_of(wide + normed(dot(jnp.concatenate(att, axis=0), out[...])))


def second_kernel(right_all, left_all, down, up, classes, w3, out, ones, lanes, srow, hr, hl):
    right, left = (
        jnp.concatenate([ref[432:].astype(F32), ref[:144].astype(F32)], axis=0)
        for ref in (right_all, left_all)
    )
    wide = windows_of(right, left)
    x = jnp.concatenate([wide.astype(BF), down[:144], up[...]], axis=0)
    q, k, v = project(x, w3, ones, srow, 576)
    got = down[144:216]
    far = jnp.concatenate([got[:, b * 128:b * 128 + 128].astype(F32) for b in range(4)], axis=0)
    far = far.astype(BF)
    att = []
    for at in (0, 144):
        span = slice(at, at + 144)
        mark = classes[576 + at:720 + at]
        att.append(heads(q[span], k[span], v[span], lanes[...], mark * lanes[2:3], mark))
    marks = (jnp.concatenate([far[144:], far[:144]], axis=0), classes[864:1152])
    for e in range(2):
        own, ext = slice(288 + e * 144, 432 + e * 144), slice(576 + e * 144, 720 + e * 144)
        keys = jnp.concatenate([k[own], k[ext]], axis=0)
        values = jnp.concatenate([v[own], v[ext]], axis=0)
        att.append(
            heads(q[own], keys, values, lanes[...], marks[e][:144] * lanes[2:3], marks[e])
        )
    hr[...], hl[...] = halves_of(wide + normed(dot(jnp.concatenate(att, axis=0), out[...])))


def feed_one(h, expand, shrink):
    grown = gelu(dot(h, expand[...])).astype(BF)
    return (h.astype(F32) + normed(dot(grown, shrink[...]))).astype(BF)


def feed_kernel(h1, h2, expand, shrink, out1, out2):
    out1[...] = feed_one(h1[...], expand, shrink)
    out2[...] = feed_one(h2[...], expand, shrink)


def feed_some_kernel(h, expand, shrink, out):
    out[...] = feed_one(h[...], expand, shrink)


def merge_kernel(l1, l2, r1, r2, pm, weight, coarse, ball, *, g):
    for half, (one, two) in enumerate(((l1, l2), (r1, r2))):
        for n, block in enumerate((two[144:], (one[:144], one[144:])[g], (one[144:], two[:144])[g])):
            ball[288 * n + half * 144:288 * n + half * 144 + 144] = block
    picked = dot(pm[g], ball[...])
    quartet = jnp.concatenate([picked[m * 144:m * 144 + 144] for m in range(4)], axis=1)
    coarse[...] = dot(normed(quartet).astype(BF), weight[...]).astype(BF)


def skip_kernel(l1, l2, r1, r2, perm, skip):
    for half, (one, two) in enumerate(((l1, l2), (r1, r2))):
        own = jnp.concatenate([two[144:], one[...], two[:144]], axis=0)
        got = dot(perm[...], own).astype(BF)
        for l in range(4):
            at = l * 288 + half * 144
            skip[at:at + 144] = got[l * 144:l * 144 + 144]


def attend_two_kernel(me, own, other, w3, ones, lanes, srow, x_out, att_out):
    a, b = own[...].astype(F32), other[...].astype(F32)
    first = me[0] == 0
    t0, t1 = jnp.where(first, a, b), jnp.where(first, b, a)
    x = jnp.concatenate([t0[:72], t1[:72], t0[72:], t1[72:]], axis=0).astype(BF)
    x_out[...] = x
    q = unit(dot_nt(x, w3[0]).astype(BF), ones[...], srow[...])
    k = unit(dot_nt(x, w3[1]).astype(BF), ones[...])
    v = dot_nt(x, w3[2]).astype(BF)
    for lg in range(2):
        span = slice(lg * 144, lg * 144 + 144)
        att_out[span] = heads(q[span], k[span], v[span], lanes[...])


def feed_two_kernel(me, x, mine, theirs, o_mine, o_theirs, expand, shrink, keep, send, hid_own):
    branch = dot(mine[...], o_mine[...]) + dot(theirs[...], o_theirs[...])
    hid = (x[...].astype(F32) + normed(branch)).astype(BF)
    acc = dot(gelu(dot_nt(hid, expand[...])).astype(BF), shrink[...])
    first = me[0] == 0

    def split(values):
        p0 = jnp.concatenate([values[0:72], values[144:216]], axis=0)
        p1 = jnp.concatenate([values[72:144], values[216:288]], axis=0)
        return jnp.where(first, p0, p1), jnp.where(first, p1, p0)

    own, far = split(acc)
    keep[...] = own
    send[...] = far.astype(BF)
    hid_own[...] = split(hid.astype(F32))[0].astype(BF)


def finish_rows(k, r, h, pout):
    done = (h[...].astype(F32) + normed(k[...] + r[...].astype(F32))).astype(BF)
    return dot(pout[...], done).reshape(6, 6, 4, 1024).astype(BF)


def finish_first_kernel(k, r, h, pout, rows):
    rows[...] = finish_rows(k, r, h, pout)


def finish_kernel(first, k, r, h, pout, coarse):
    coarse[:6] = first[...]
    coarse[6:] = finish_rows(k, r, h, pout)


def behind(value, axis, steps):
    count = lax.axis_size(axis)
    return lax.ppermute(value, axis, [(s, (s + steps) % count) for s in range(count)])


def after(value, done):
    return lax.optimization_barrier((value, done))[0]


def across(value, axis, flip):
    return lax.ppermute(value, axis, [(s, s ^ flip) for s in range(lax.axis_size(axis))])


def shards(
    patches,
    region_ids,
    triple_one,
    output_one,
    expand_one,
    shrink_one,
    scales_one,
    merge_weight,
    triple_two,
    output_two,
    expand_two,
    shrink_two,
    scales_two,
):
    me = lax.axis_index("tp").astype(jnp.int32).reshape(1)
    lat_at = (lax.axis_index("lat") & 3).astype(jnp.int32).reshape(1)
    ones = const(np.kron(np.eye(4), np.ones((64, 64))))
    lane_of = np.zeros((8, 128), np.float32)
    lane_of[0, :64] = 1
    lane_of[1, 64:] = 1
    lane_of[2] = MASK
    lane_of[2, 8] = -MASK
    lanes = const(lane_of)
    spread = const(np.kron(np.eye(8), np.ones((1, 64))))
    col_axes = ("lon", "tp")
    tok = lambda n: ((n, 512), BF)

    flat = patches.transpose(0, 2, 1, 3).reshape(1152, 512)
    left, right = call(
        pack_kernel,
        [tok(576)] * 2,
        [flat],
        10**9,
    )
    region_ids = after(region_ids, right)
    left = behind(left, col_axes, -1)
    pick, keep = pick_rows()
    classes, s_one, s_two, quarter = call(
        ready_kernel,
        [((1152, 128), BF), ((1, 512), F32), ((1, 512), F32), ((128, 1024), BF)],
        [
            lat_at,
            region_ids.transpose(2, 0, 1),
            const(pick),
            const(keep),
            scales_one.reshape(1, 8),
            scales_two.reshape(1, 8),
            spread,
            output_two,
        ],
        10**9,
        smem=(0,),
        hbm=(7,),
        scratch=[pltpu.SemaphoreType.DMA],
    )
    quarter = after(quarter, left)
    oa = behind(quarter, "tp", 1)
    down, up = call(rim_kernel, [tok(216), tok(144)], [left, right, classes], 10**6)
    classes = after(classes, down)
    down, up = behind(down, "lat", 1), behind(up, "lat", -1)

    w_one = triple_one.transpose(1, 0, 2)
    shared = [classes, w_one, output_one, ones, lanes, s_one]
    hr1, hl1 = call(first_kernel, [tok(288)] * 2, [right, left] + shared, 4 * 10**9)
    hl1 = behind(hl1, col_axes, 1)
    shared[0] = after(classes, (hr1, oa))
    hr2, hl2 = call(
        second_kernel, [tok(288)] * 2, [right, left, down, up] + shared, 6 * 10**9
    )
    hl2 = behind(hl2, col_axes, 1)

    feeds = [expand_one, shrink_one]
    br1, br2 = call(feed_kernel, [tok(288)] * 2, [hr1, hr2] + feeds, 3 * 10**9)
    bl1 = call(feed_some_kernel, [tok(288)], [after(hl1, br1)] + feeds, 2 * 10**9)[0]
    oa = after(oa, bl1)
    ob, oc = across(oa, "lat", 1), across(oa, "lat", 2)
    bl2 = call(feed_some_kernel, [tok(288)], [after(hl2, bl1)] + feeds, 2 * 10**9)[0]
    blocks = [bl1, bl2, br1, br2]
    od = across(after(oc, bl2), "lat", 1)
    pm, coarse_in = const(merge_rows()), []
    for g in range(2):
        if g:
            blocks = [after(blocks[0], coarse_in[0])] + blocks[1:]
        coarse_in += call(
            functools.partial(merge_kernel, g=g),
            [((144, 1024), BF)],
            blocks + [pm, merge_weight],
            10**9,
            scratch=[pltpu.VMEM((864, 512), BF)],
        )
    c0, c1 = coarse_in
    d0, d1 = behind(c0, "tp", 1), behind(c1, "tp", 1)
    blocks[0], od = after(blocks[0], c1), after(od, c1)
    skip = call(skip_kernel, [tok(1152)], blocks + [const(home_rows())], 2 * 10**9)[0]
    o_theirs = call(
        join_kernel, [((512, 1024), BF)], [lat_at, oa, ob, oc, od], 10**9, smem=(0,)
    )[0]
    c0, skip, o_theirs = lax.optimization_barrier((c0, skip, o_theirs))
    skip = skip.reshape(4, 12, 24, 512).transpose(0, 2, 1, 3)

    w_two = triple_two.transpose(1, 0, 2)
    attended = []
    for own, other in ((c0, d0), (c1, d1)):
        if attended:
            own = after(own, attended[0][1])
        x, mine = call(
            attend_two_kernel,
            [((288, 1024), BF), tok(288)],
            [me, own, other, w_two, ones, lanes, s_two],
            2 * 10**9,
            smem=(0,),
        )
        attended.append((x, mine, behind(mine, "tp", 1)))
    kept = []
    for x, mine, theirs in attended:
        if kept:
            x = after(x, kept[0][0])
        keep, send, hid_own = call(
            feed_two_kernel,
            [((144, 1024), F32), ((144, 1024), BF), ((144, 1024), BF)],
            [me, x, mine, theirs, output_two, o_theirs, expand_two, shrink_two],
            10**8,
            smem=(0,),
        )
        kept.append((keep, behind(send, "tp", 1), hid_own))
    pout = const(coarse_rows())
    first = call(finish_first_kernel, [((6, 6, 4, 1024), BF)], [*kept[0], pout], 10**8)[0]
    coarse = call(finish_kernel, [((12, 6, 4, 1024), BF)], [first, *kept[1], pout], 10**8)[0]
    return (skip, coarse.transpose(2, 0, 1, 3))


def solution(mesh):
    in_specs = (
        P(None, "lat", ("lon", "tp"), None),
        P(None, "lat", ("lon", "tp")),
        P(),
        P(),
        P(),
        P(),
        P(),
        P(),
        P("tp", None, None),
        P("tp", None),
        P("tp", None),
        P("tp", None),
        P("tp"),
    )
    out_specs = (P(None, "lat", ("lon", "tp"), None), P(None, "lat", ("lon", "tp"), None))
    return jax.shard_map(shards, mesh=mesh, in_specs=in_specs, out_specs=out_specs, check_vma=False)
```

```python
import functools
import math

import jax
import jax.numpy as jnp
import numpy as np
from jax import lax
from jax.experimental import pallas as pl
from jax.experimental.pallas import tpu as pltpu
from jax.sharding import PartitionSpec as P

BF = jnp.bfloat16
F32 = jnp.float32
MASK = 192.0
LOG2E = math.log2(math.e)
MIB = 1024 * 1024


def home_level(lg, l):
    return (2 * lg + l + 1) % 4


def pick_rows():
    rows, keep = np.zeros((1152, 48), np.float32), np.zeros((1152, 24), np.float32)
    group = np.zeros((1152, 1), np.float32)
    at = 0
    for w in range(4):
        for part in range(2 if w == 3 else 1):
            outer = [(h, g) for h in range(2) for g in range(2)]
            if w < 3:
                outer = [(h, g) for g in range(2) for h in range(2)]
            for half, lg in outer:
                for l in range(2):
                    for i in range(3 * part, 3 * part + 3) if w == 3 else range(6):
                        for j in range(6):
                            rows[at, (half * 6 + j) * 4 + 2 * lg + l] = 1
                            keep[at, 6 * w + i] = 1
                            group[at] = 4 * lg
                            at += 1
    return rows, np.concatenate([keep, group], axis=1)


def place(level, i, j):
    lg, l = ((level - 1) % 4) // 2, ((level - 1) % 4) % 2
    if i < 3 or i >= 21:
        edge, ie = (0, i) if i < 3 else (1, i - 21)
        return edge * 72 + lg * 36 + l * 18 + ie * 6 + j
    w, iw = (i - 3) // 6, (i - 3) % 6
    return 144 + w * 144 + lg * 72 + l * 36 + iw * 6 + j


def home_rows():
    mat = np.zeros((576, 576), np.float32)
    for level in range(4):
        for j in range(6):
            for i in range(24):
                mat[level * 144 + j * 24 + i, place(level, i, j)] = 1
    return mat


def merge_rows():
    mat = np.zeros((2, 4, 144, 864), np.float32)
    for g in range(2):
        for m in range(4):
            pi, pj = m // 2, m % 2
            for level in range(4):
                for ii in range(6):
                    i = 2 * (6 * g + ii) + pi
                    for jj in range(6):
                        half, j = jj // 3, 2 * (jj % 3) + pj
                        at = place(level, i, j)
                        chunk = 0 if at < 144 else at // 144 - g
                        row = (level // 2) * 72 + (level % 2) * 36 + ii * 6 + jj
                        mat[g, m, row, 288 * chunk + half * 144 + at % 144] = 1
    return mat.reshape(2, 576, 864)


def coarse_rows():
    mat = np.zeros((144, 144), np.float32)
    for level in range(4):
        for ii in range(6):
            for jj in range(6):
                row = (ii * 6 + jj) * 4 + level
                mat[row, (level // 2) * 72 + (level % 2) * 36 + ii * 6 + jj] = 1
    return mat


def const(mat):
    return jnp.asarray(mat, dtype=BF)


def dot(a, b):
    return lax.dot_general(a, b, (((1,), (0,)), ((), ())), preferred_element_type=F32)


def dot_nt(a, b):
    return lax.dot_general(a, b, (((1,), (1,)), ((), ())), preferred_element_type=F32)


def normed(values):
    centred = values - jnp.mean(values, axis=-1, keepdims=True)
    spread = jnp.mean(centred * centred, axis=-1, keepdims=True)
    return centred * lax.rsqrt(spread + 1e-05)


def gelu(x):
    x = x.astype(BF)
    inner = x * (jnp.asarray(0.7978845608, BF) + jnp.asarray(0.0356774081, BF) * (x * x))
    return (x * jnp.asarray(0.5, BF)) * (jnp.asarray(1.0, BF) + jnp.tanh(inner))


def unit(packed, ones, factor=None):
    wide = packed.astype(F32)
    squares = (wide * wide).astype(BF)
    total = jnp.concatenate([dot(squares[:, :256], ones), dot(squares[:, 256:], ones)], axis=1)
    result = wide * lax.rsqrt(total + 1e-06)
    if factor is not None:
        result = result * factor
    return result.astype(BF)


def heads(q, k, v, lanes, aug_q=None, aug_k=None):
    count = q.shape[0]
    low, high = lanes[0:1], lanes[1:2]
    first = lax.broadcasted_iota(jnp.int32, (count, 128), 1) < 64
    if aug_q is not None:
        aug_q = jnp.concatenate([aug_q, aug_q], axis=0)
    ones = jnp.ones((v.shape[0], 128), BF)
    parts = []
    for pair in range(4):
        span = slice(pair * 128, pair * 128 + 128)
        qp, kp = q[:, span], k[:, span]
        qp = jnp.concatenate([qp * low, qp * high], axis=0)
        if aug_q is not None:
            qp = jnp.concatenate([qp, aug_q], axis=1)
            kp = jnp.concatenate([kp, aug_k], axis=1)
        weights = jnp.exp2(dot_nt(qp, kp)).astype(BF)
        acc = dot(weights, jnp.concatenate([v[:, span], ones], axis=1))
        both = jnp.where(first, acc[:count, :128], acc[count:, :128])
        total = jnp.where(first, acc[:count, 128:], acc[count:, 128:])
        parts.append(both / total)
    return jnp.concatenate(parts, axis=1).astype(BF)


def call(kernel, outs, args, flops, vmem=16, smem=(), hbm=(), scratch=()):
    def space(n):
        return pltpu.SMEM if n in smem else pltpu.HBM if n in hbm else pltpu.VMEM

    moved = sum(int(np.prod(a.shape)) * a.dtype.itemsize for a in args)
    return pl.pallas_call(
        kernel,
        out_shape=[jax.ShapeDtypeStruct(shape, kind) for shape, kind in outs],
        in_specs=[pl.BlockSpec(memory_space=space(n)) for n in range(len(args))],
        out_specs=[pl.BlockSpec(memory_space=pltpu.VMEM) for _ in outs],
        scratch_shapes=list(scratch),
        compiler_params=pltpu.CompilerParams(vmem_limit_bytes=vmem * MIB),
        cost_estimate=pl.CostEstimate(flops=flops, bytes_accessed=moved, transcendentals=0),
    )(*args)


def pack_kernel(x, left, right):
    row = lax.broadcasted_iota(jnp.int32, (144, 144), 0)
    col = lax.broadcasted_iota(jnp.int32, (144, 144), 1)
    six = (row * 10923) >> 16
    lat = jnp.where(row < 18, six, jnp.where(row < 36, six + 18, six - 3))
    perm = jnp.where(col == (row - 6 * six) * 24 + lat, 1.0, 0.0).astype(BF)
    for half, dst in enumerate((left, right)):
        got = []
        for level in (1, 2, 3, 0):
            at = level * 288 + half * 144
            got.append(dot(perm, x[at:at + 144]))
        rows = [g[e:e + 18] for e in (0, 18) for g in got]
        dst[:144] = jnp.concatenate(rows, axis=0).astype(BF)
        rows = [g[w:w + 36] for w in (36, 72, 108) for g in got]
        dst[144:] = jnp.concatenate(rows, axis=0).astype(BF)


def ready_kernel(
    at, ids, rows, keep, sone, stwo, spread, o_two, classes, s_one, s_two, quarter, sem
):
    copy = pltpu.make_async_copy(
        o_two.at[pl.ds(pl.multiple_of(at[0] * 128, 128), 128)], quarter, sem
    )
    copy.start()
    for src, dst in ((sone, s_one), (stwo, s_two)):
        dst[...] = dot(src[...], spread[...])[0:1] * LOG2E
    grid = jnp.concatenate([ids[c] for c in range(12)], axis=0).astype(F32).astype(BF)
    picked = jnp.concatenate([dot(rows[...], grid), jnp.ones((1152, 1), F32)], axis=1)
    name = jnp.sum(picked * keep[...].astype(F32), axis=1, keepdims=True)
    lane = lax.broadcasted_iota(jnp.int32, (1152, 128), 1)
    hit = (lane.astype(F32) == name) | (lane == 8)
    classes[...] = jnp.where(hit, 1.0, 0.0).astype(BF)
    copy.wait()


def rim_kernel(left_all, right_all, classes, down, up):
    left, right = left_all[:144].astype(F32), right_all[:144].astype(F32)
    marks = classes[864:].astype(F32)
    up[...] = jnp.concatenate([right[:72], left[:72]], axis=0).astype(BF)
    wide = jnp.concatenate([marks[b * 72:b * 72 + 72] for b in range(4)], axis=1)
    down[...] = jnp.concatenate([right[72:], left[72:], wide], axis=0).astype(BF)


def join_kernel(at, a, b, c, d, out):
    mine = at[0]
    for step, part in enumerate((a, b, c, d)):
        out[pl.ds(pl.multiple_of((mine ^ step) * 128, 128), 128)] = part[...]


def windows_of(right, left):
    parts = []
    for at in range(0, right.shape[0], 72):
        parts += [right[at:at + 72], left[at:at + 72]]
    return jnp.concatenate(parts, axis=0)


def halves_of(rows):
    right = [rows[at:at + 72] for at in range(0, rows.shape[0], 144)]
    left = [rows[at + 72:at + 144] for at in range(0, rows.shape[0], 144)]
    return jnp.concatenate(right, axis=0).astype(BF), jnp.concatenate(left, axis=0).astype(BF)


def project(x, w3, ones, srow, first=None):
    q = unit(dot_nt(x[:first], w3[0]).astype(BF), ones[...], srow[...])
    k = unit(dot_nt(x, w3[1]).astype(BF), ones[...])
    return q, k, dot_nt(x, w3[2]).astype(BF)


def first_kernel(right, left, classes, w3, out, ones, lanes, srow, hr, hl):
    wide = windows_of(right[144:432].astype(F32), left[144:432].astype(F32))
    q, k, v = project(wide.astype(BF), w3, ones, srow)
    att = []
    for at in range(0, 576, 144):
        span = slice(at, at + 144)
        mark = classes[span]
        att.append(heads(q[span], k[span], v[span], lanes[...], mark * lanes[2:3], mark))
    hr[...], hl[...] = halves_of(wide + normed(dot(jnp.concatenate(att, axis=0), out[...])))


def second_kernel(right_all, left_all, down, up, classes, w3, out, ones, lanes, srow, hr, hl):
    right, left = (
        jnp.concatenate([ref[432:].astype(F32), ref[:144].astype(F32)], axis=0)
        for ref in (right_all, left_all)
    )
    wide = windows_of(right, left)
    x = jnp.concatenate([wide.astype(BF), down[:144], up[...]], axis=0)
    q, k, v = project(x, w3, ones, srow, 576)
    got = down[144:216]
    far = jnp.concatenate([got[:, b * 128:b * 128 + 128].astype(F32) for b in range(4)], axis=0)
    far = far.astype(BF)
    att = []
    for at in (0, 144):
        span = slice(at, at + 144)
        mark = classes[576 + at:720 + at]
        att.append(heads(q[span], k[span], v[span], lanes[...], mark * lanes[2:3], mark))
    marks = (jnp.concatenate([far[144:], far[:144]], axis=0), classes[864:1152])
    for e in range(2):
        own, ext = slice(288 + e * 144, 432 + e * 144), slice(576 + e * 144, 720 + e * 144)
        keys = jnp.concatenate([k[own], k[ext]], axis=0)
        values = jnp.concatenate([v[own], v[ext]], axis=0)
        att.append(
            heads(q[own], keys, values, lanes[...], marks[e][:144] * lanes[2:3], marks[e])
        )
    hr[...], hl[...] = halves_of(wide + normed(dot(jnp.concatenate(att, axis=0), out[...])))


def feed_one(h, expand, shrink):
    grown = gelu(dot(h, expand[...])).astype(BF)
    return (h.astype(F32) + normed(dot(grown, shrink[...]))).astype(BF)


def feed_kernel(h1, h2, expand, shrink, out1, out2):
    out1[...] = feed_one(h1[...], expand, shrink)
    out2[...] = feed_one(h2[...], expand, shrink)


def feed_some_kernel(h, expand, shrink, out):
    out[...] = feed_one(h[...], expand, shrink)


def merge_kernel(l1, l2, r1, r2, pm, weight, coarse, ball, *, g):
    for half, (one, two) in enumerate(((l1, l2), (r1, r2))):
        for n, block in enumerate((two[144:], (one[:144], one[144:])[g], (one[144:], two[:144])[g])):
            ball[288 * n + half * 144:288 * n + half * 144 + 144] = block
    picked = dot(pm[g], ball[...])
    quartet = jnp.concatenate([picked[m * 144:m * 144 + 144] for m in range(4)], axis=1)
    coarse[...] = dot(normed(quartet).astype(BF), weight[...]).astype(BF)


def skip_kernel(l1, l2, r1, r2, perm, skip):
    for half, (one, two) in enumerate(((l1, l2), (r1, r2))):
        own = jnp.concatenate([two[144:], one[...], two[:144]], axis=0)
        got = dot(perm[...], own).astype(BF)
        for l in range(4):
            at = l * 288 + half * 144
            skip[at:at + 144] = got[l * 144:l * 144 + 144]


def attend_two_kernel(me, own, other, w3, ones, lanes, srow, x_out, att_out):
    a, b = own[...].astype(F32), other[...].astype(F32)
    first = me[0] == 0
    t0, t1 = jnp.where(first, a, b), jnp.where(first, b, a)
    x = jnp.concatenate([t0[:72], t1[:72], t0[72:], t1[72:]], axis=0).astype(BF)
    x_out[...] = x
    q = unit(dot_nt(x, w3[0]).astype(BF), ones[...], srow[...])
    k = unit(dot_nt(x, w3[1]).astype(BF), ones[...])
    v = dot_nt(x, w3[2]).astype(BF)
    for lg in range(2):
        span = slice(lg * 144, lg * 144 + 144)
        att_out[span] = heads(q[span], k[span], v[span], lanes[...])


def feed_two_kernel(me, x, mine, theirs, o_mine, o_theirs, expand, shrink, keep, send, hid_own):
    branch = dot(mine[...], o_mine[...]) + dot(theirs[...], o_theirs[...])
    hid = (x[...].astype(F32) + normed(branch)).astype(BF)
    acc = dot(gelu(dot_nt(hid, expand[...])).astype(BF), shrink[...])
    first = me[0] == 0

    def split(values):
        p0 = jnp.concatenate([values[0:72], values[144:216]], axis=0)
        p1 = jnp.concatenate([values[72:144], values[216:288]], axis=0)
        return jnp.where(first, p0, p1), jnp.where(first, p1, p0)

    own, far = split(acc)
    keep[...] = own
    send[...] = far.astype(BF)
    hid_own[...] = split(hid.astype(F32))[0].astype(BF)


def finish_rows(k, r, h, pout):
    done = (h[...].astype(F32) + normed(k[...] + r[...].astype(F32))).astype(BF)
    return dot(pout[...], done).reshape(6, 6, 4, 1024).astype(BF)


def finish_first_kernel(k, r, h, pout, rows):
    rows[...] = finish_rows(k, r, h, pout)


def finish_kernel(first, k, r, h, pout, coarse):
    coarse[:6] = first[...]
    coarse[6:] = finish_rows(k, r, h, pout)


def behind(value, axis, steps):
    count = lax.axis_size(axis)
    return lax.ppermute(value, axis, [(s, (s + steps) % count) for s in range(count)])


def after(value, done):
    return lax.optimization_barrier((value, done))[0]


def across(value, axis, flip):
    return lax.ppermute(value, axis, [(s, s ^ flip) for s in range(lax.axis_size(axis))])


def shards(
    patches,
    region_ids,
    triple_one,
    output_one,
    expand_one,
    shrink_one,
    scales_one,
    merge_weight,
    triple_two,
    output_two,
    expand_two,
    shrink_two,
    scales_two,
):
    me = lax.axis_index("tp").astype(jnp.int32).reshape(1)
    lat_at = (lax.axis_index("lat") & 3).astype(jnp.int32).reshape(1)
    ones = const(np.kron(np.eye(4), np.ones((64, 64))))
    lane_of = np.zeros((8, 128), np.float32)
    lane_of[0, :64] = 1
    lane_of[1, 64:] = 1
    lane_of[2] = MASK
    lane_of[2, 8] = -MASK
    lanes = const(lane_of)
    spread = const(np.kron(np.eye(8), np.ones((1, 64))))
    col_axes = ("lon", "tp")
    tok = lambda n: ((n, 512), BF)

    flat = patches.transpose(0, 2, 1, 3).reshape(1152, 512)
    left, right = call(
        pack_kernel,
        [tok(576)] * 2,
        [flat],
        10**9,
    )
    region_ids = after(region_ids, right)
    left = behind(left, col_axes, -1)
    pick, keep = pick_rows()
    classes, s_one, s_two, quarter = call(
        ready_kernel,
        [((1152, 128), BF), ((1, 512), F32), ((1, 512), F32), ((128, 1024), BF)],
        [
            lat_at,
            region_ids.transpose(2, 0, 1),
            const(pick),
            const(keep),
            scales_one.reshape(1, 8),
            scales_two.reshape(1, 8),
            spread,
            output_two,
        ],
        10**9,
        smem=(0,),
        hbm=(7,),
        scratch=[pltpu.SemaphoreType.DMA],
    )
    quarter = after(quarter, left)
    oa = behind(quarter, "tp", 1)
    down, up = call(rim_kernel, [tok(216), tok(144)], [left, right, classes], 10**6)
    classes = after(classes, down)
    down, up = behind(down, "lat", 1), behind(up, "lat", -1)

    w_one = triple_one.transpose(1, 0, 2)
    shared = [classes, w_one, output_one, ones, lanes, s_one]
    hr1, hl1 = call(first_kernel, [tok(288)] * 2, [right, left] + shared, 4 * 10**9)
    hl1 = behind(hl1, col_axes, 1)
    shared[0] = after(classes, (hr1, oa))
    hr2, hl2 = call(
        second_kernel, [tok(288)] * 2, [right, left, down, up] + shared, 6 * 10**9
    )
    hl2 = behind(hl2, col_axes, 1)

    feeds = [expand_one, shrink_one]
    br1, br2 = call(feed_kernel, [tok(288)] * 2, [hr1, hr2] + feeds, 3 * 10**9)
    bl1 = call(feed_some_kernel, [tok(288)], [after(hl1, br1)] + feeds, 2 * 10**9)[0]
    oa = after(oa, bl1)
    ob, oc = across(oa, "lat", 1), across(oa, "lat", 2)
    bl2 = call(feed_some_kernel, [tok(288)], [after(hl2, bl1)] + feeds, 2 * 10**9)[0]
    blocks = [bl1, bl2, br1, br2]
    od = across(after(oc, bl2), "lat", 1)
    pm, coarse_in = const(merge_rows()), []
    for g in range(2):
        if g:
            blocks = [after(blocks[0], coarse_in[0])] + blocks[1:]
        coarse_in += call(
            functools.partial(merge_kernel, g=g),
            [((144, 1024), BF)],
            blocks + [pm, merge_weight],
            10**9,
            scratch=[pltpu.VMEM((864, 512), BF)],
        )
    c0, c1 = coarse_in
    d0, d1 = behind(c0, "tp", 1), behind(c1, "tp", 1)
    blocks[0], od = after(blocks[0], c1), after(od, c1)
    skip = call(skip_kernel, [tok(1152)], blocks + [const(home_rows())], 2 * 10**9)[0]
    o_theirs = call(
        join_kernel, [((512, 1024), BF)], [lat_at, oa, ob, oc, od], 10**9, smem=(0,)
    )[0]
    c0, skip, o_theirs = lax.optimization_barrier((c0, skip, o_theirs))
    skip = skip.reshape(4, 12, 24, 512).transpose(0, 2, 1, 3)

    w_two = triple_two.transpose(1, 0, 2)
    attended = []
    for own, other in ((c0, d0), (c1, d1)):
        if attended:
            own = after(own, attended[0][1])
        x, mine = call(
            attend_two_kernel,
            [((288, 1024), BF), tok(288)],
            [me, own, other, w_two, ones, lanes, s_two],
            2 * 10**9,
            smem=(0,),
        )
        attended.append((x, mine, behind(mine, "tp", 1)))
    kept = []
    for x, mine, theirs in attended:
        if kept:
            x = after(x, kept[0][0])
        keep, send, hid_own = call(
            feed_two_kernel,
            [((144, 1024), F32), ((144, 1024), BF), ((144, 1024), BF)],
            [me, x, mine, theirs, output_two, o_theirs, expand_two, shrink_two],
            10**8,
            smem=(0,),
        )
        kept.append((keep, behind(send, "tp", 1), hid_own))
    pout = const(coarse_rows())
    first = call(finish_first_kernel, [((6, 6, 4, 1024), BF)], [*kept[0], pout], 10**8)[0]
    coarse = call(finish_kernel, [((12, 6, 4, 1024), BF)], [first, *kept[1], pout], 10**8)[0]
    return (skip, coarse.transpose(2, 0, 1, 3))


def solution(mesh):
    in_specs = (
        P(None, "lat", ("lon", "tp"), None),
        P(None, "lat", ("lon", "tp")),
        P(),
        P(),
        P(),
        P(),
        P(),
        P(),
        P("tp", None, None),
        P("tp", None),
        P("tp", None),
        P("tp", None),
        P("tp"),
    )
    out_specs = (P(None, "lat", ("lon", "tp"), None), P(None, "lat", ("lon", "tp"), None))
    return jax.shard_map(shards, mesh=mesh, in_specs=in_specs, out_specs=out_specs, check_vma=False)
```

```python
import functools
import math

import jax
import jax.numpy as jnp
import numpy as np
from jax import lax
from jax.experimental import pallas as pl
from jax.experimental.pallas import tpu as pltpu
from jax.sharding import PartitionSpec as P

BF = jnp.bfloat16
F32 = jnp.float32
MASK = 192.0
LOG2E = math.log2(math.e)
MIB = 1024 * 1024


def home_level(lg, l):
    return (2 * lg + l + 1) % 4


def pick_rows():
    rows, keep = np.zeros((1152, 48), np.float32), np.zeros((1152, 24), np.float32)
    group = np.zeros((1152, 1), np.float32)
    at = 0
    for w in range(4):
        for part in range(2 if w == 3 else 1):
            outer = [(h, g) for h in range(2) for g in range(2)]
            if w < 3:
                outer = [(h, g) for g in range(2) for h in range(2)]
            for half, lg in outer:
                for l in range(2):
                    for i in range(3 * part, 3 * part + 3) if w == 3 else range(6):
                        for j in range(6):
                            rows[at, (half * 6 + j) * 4 + 2 * lg + l] = 1
                            keep[at, 6 * w + i] = 1
                            group[at] = 4 * lg
                            at += 1
    return rows, np.concatenate([keep, group], axis=1)


def place(level, i, j):
    lg, l = ((level - 1) % 4) // 2, ((level - 1) % 4) % 2
    if i < 3 or i >= 21:
        edge, ie = (0, i) if i < 3 else (1, i - 21)
        return edge * 72 + lg * 36 + l * 18 + ie * 6 + j
    w, iw = (i - 3) // 6, (i - 3) % 6
    return 144 + w * 144 + lg * 72 + l * 36 + iw * 6 + j


def home_rows():
    mat = np.zeros((576, 576), np.float32)
    for level in range(4):
        for j in range(6):
            for i in range(24):
                mat[level * 144 + j * 24 + i, place(level, i, j)] = 1
    return mat


def merge_rows():
    mat = np.zeros((2, 4, 144, 864), np.float32)
    for g in range(2):
        for m in range(4):
            pi, pj = m // 2, m % 2
            for level in range(4):
                for ii in range(6):
                    i = 2 * (6 * g + ii) + pi
                    for jj in range(6):
                        half, j = jj // 3, 2 * (jj % 3) + pj
                        at = place(level, i, j)
                        chunk = 0 if at < 144 else at // 144 - g
                        row = (level // 2) * 72 + (level % 2) * 36 + ii * 6 + jj
                        mat[g, m, row, 288 * chunk + half * 144 + at % 144] = 1
    return mat.reshape(2, 576, 864)


def coarse_rows():
    mat = np.zeros((144, 144), np.float32)
    for level in range(4):
        for ii in range(6):
            for jj in range(6):
                row = (ii * 6 + jj) * 4 + level
                mat[row, (level // 2) * 72 + (level % 2) * 36 + ii * 6 + jj] = 1
    return mat


def const(mat):
    return jnp.asarray(mat, dtype=BF)


def dot(a, b):
    return lax.dot_general(a, b, (((1,), (0,)), ((), ())), preferred_element_type=F32)


def dot_nt(a, b):
    return lax.dot_general(a, b, (((1,), (1,)), ((), ())), preferred_element_type=F32)


def normed(values):
    centred = values - jnp.mean(values, axis=-1, keepdims=True)
    spread = jnp.mean(centred * centred, axis=-1, keepdims=True)
    return centred * lax.rsqrt(spread + 1e-05)


def gelu(x):
    x = x.astype(BF)
    inner = x * (jnp.asarray(0.7978845608, BF) + jnp.asarray(0.0356774081, BF) * (x * x))
    return (x * jnp.asarray(0.5, BF)) * (jnp.asarray(1.0, BF) + jnp.tanh(inner))


def unit(packed, ones, factor=None):
    wide = packed.astype(F32)
    squares = (wide * wide).astype(BF)
    total = jnp.concatenate([dot(squares[:, :256], ones), dot(squares[:, 256:], ones)], axis=1)
    result = wide * lax.rsqrt(total + 1e-06)
    if factor is not None:
        result = result * factor
    return result.astype(BF)


def heads(q, k, v, lanes, aug_q=None, aug_k=None):
    count = q.shape[0]
    low, high = lanes[0:1], lanes[1:2]
    first = lax.broadcasted_iota(jnp.int32, (count, 128), 1) < 64
    if aug_q is not None:
        aug_q = jnp.concatenate([aug_q, aug_q], axis=0)
    ones = jnp.ones((v.shape[0], 128), BF)
    parts = []
    for pair in range(4):
        span = slice(pair * 128, pair * 128 + 128)
        qp, kp = q[:, span], k[:, span]
        qp = jnp.concatenate([qp * low, qp * high], axis=0)
        if aug_q is not None:
            qp = jnp.concatenate([qp, aug_q], axis=1)
            kp = jnp.concatenate([kp, aug_k], axis=1)
        weights = jnp.exp2(dot_nt(qp, kp)).astype(BF)
        acc = dot(weights, jnp.concatenate([v[:, span], ones], axis=1))
        both = jnp.where(first, acc[:count, :128], acc[count:, :128])
        total = jnp.where(first, acc[:count, 128:], acc[count:, 128:])
        parts.append(both / total)
    return jnp.concatenate(parts, axis=1).astype(BF)


def call(kernel, outs, args, flops, vmem=16, smem=(), hbm=(), scratch=()):
    def space(n):
        return pltpu.SMEM if n in smem else pltpu.HBM if n in hbm else pltpu.VMEM

    moved = sum(int(np.prod(a.shape)) * a.dtype.itemsize for a in args)
    return pl.pallas_call(
        kernel,
        out_shape=[jax.ShapeDtypeStruct(shape, kind) for shape, kind in outs],
        in_specs=[pl.BlockSpec(memory_space=space(n)) for n in range(len(args))],
        out_specs=[pl.BlockSpec(memory_space=pltpu.VMEM) for _ in outs],
        scratch_shapes=list(scratch),
        compiler_params=pltpu.CompilerParams(vmem_limit_bytes=vmem * MIB),
        cost_estimate=pl.CostEstimate(flops=flops, bytes_accessed=moved, transcendentals=0),
    )(*args)


def pack_kernel(x, out):
    row = lax.broadcasted_iota(jnp.int32, (144, 144), 0)
    col = lax.broadcasted_iota(jnp.int32, (144, 144), 1)
    six = (row * 10923) >> 16
    lat = jnp.where(row < 18, six, jnp.where(row < 36, six + 18, six - 3))
    perm = jnp.where(col == (row - 6 * six) * 24 + lat, 1.0, 0.0).astype(BF)
    got = [dot(perm, x[level]) for level in (1, 2, 3, 0)]
    rows = [g[e:e + 18] for e in (0, 18) for g in got]
    out[:144] = jnp.concatenate(rows, axis=0).astype(BF)
    rows = [g[w:w + 36] for w in (36, 72, 108) for g in got]
    out[144:] = jnp.concatenate(rows, axis=0).astype(BF)


def ready_kernel(
    at, ids, rows, keep, sone, stwo, spread, o_two, classes, s_one, s_two, quarter, sem
):
    copy = pltpu.make_async_copy(
        o_two.at[pl.ds(pl.multiple_of(at[0] * 128, 128), 128)], quarter, sem
    )
    copy.start()
    for src, dst in ((sone, s_one), (stwo, s_two)):
        dst[...] = dot(src[...], spread[...])[0:1] * LOG2E
    grid = jnp.concatenate([ids[c] for c in range(12)], axis=0).astype(F32).astype(BF)
    picked = jnp.concatenate([dot(rows[...], grid), jnp.ones((1152, 1), F32)], axis=1)
    name = jnp.sum(picked * keep[...].astype(F32), axis=1, keepdims=True)
    lane = lax.broadcasted_iota(jnp.int32, (1152, 128), 1)
    hit = (lane.astype(F32) == name) | (lane == 8)
    classes[...] = jnp.where(hit, 1.0, 0.0).astype(BF)
    copy.wait()


def rim_kernel(left_all, right_all, classes, down, up):
    left, right = left_all[:144].astype(F32), right_all[:144].astype(F32)
    marks = classes[864:].astype(F32)
    up[...] = jnp.concatenate([right[:72], left[:72]], axis=0).astype(BF)
    wide = jnp.concatenate([marks[b * 72:b * 72 + 72] for b in range(4)], axis=1)
    down[...] = jnp.concatenate([right[72:], left[72:], wide], axis=0).astype(BF)


def join_kernel(at, a, b, c, d, out):
    mine = at[0]
    for step, part in enumerate((a, b, c, d)):
        out[pl.ds(pl.multiple_of((mine ^ step) * 128, 128), 128)] = part[...]


def windows_of(right, left):
    parts = []
    for at in range(0, right.shape[0], 72):
        parts += [right[at:at + 72], left[at:at + 72]]
    return jnp.concatenate(parts, axis=0)


def halves_of(rows):
    right = [rows[at:at + 72] for at in range(0, rows.shape[0], 144)]
    left = [rows[at + 72:at + 144] for at in range(0, rows.shape[0], 144)]
    return jnp.concatenate(right, axis=0).astype(BF), jnp.concatenate(left, axis=0).astype(BF)


def project(x, w3, ones, srow, first=None):
    q = unit(dot_nt(x[:first], w3[0]).astype(BF), ones[...], srow[...])
    k = unit(dot_nt(x, w3[1]).astype(BF), ones[...])
    return q, k, dot_nt(x, w3[2]).astype(BF)


def first_kernel(right, left, classes, w3, out, ones, lanes, srow, hr, hl):
    wide = windows_of(right[144:432].astype(F32), left[144:432].astype(F32))
    q, k, v = project(wide.astype(BF), w3, ones, srow)
    att = []
    for at in range(0, 576, 144):
        span = slice(at, at + 144)
        mark = classes[span]
        att.append(heads(q[span], k[span], v[span], lanes[...], mark * lanes[2:3], mark))
    hr[...], hl[...] = halves_of(wide + normed(dot(jnp.concatenate(att, axis=0), out[...])))


def second_kernel(right_all, left_all, down, up, classes, w3, out, ones, lanes, srow, hr, hl):
    right, left = (
        jnp.concatenate([ref[432:].astype(F32), ref[:144].astype(F32)], axis=0)
        for ref in (right_all, left_all)
    )
    wide = windows_of(right, left)
    x = jnp.concatenate([wide.astype(BF), down[:144], up[...]], axis=0)
    q, k, v = project(x, w3, ones, srow, 576)
    got = down[144:216]
    far = jnp.concatenate([got[:, b * 128:b * 128 + 128].astype(F32) for b in range(4)], axis=0)
    far = far.astype(BF)
    att = []
    for at in (0, 144):
        span = slice(at, at + 144)
        mark = classes[576 + at:720 + at]
        att.append(heads(q[span], k[span], v[span], lanes[...], mark * lanes[2:3], mark))
    marks = (jnp.concatenate([far[144:], far[:144]], axis=0), classes[864:1152])
    for e in range(2):
        own, ext = slice(288 + e * 144, 432 + e * 144), slice(576 + e * 144, 720 + e * 144)
        keys = jnp.concatenate([k[own], k[ext]], axis=0)
        values = jnp.concatenate([v[own], v[ext]], axis=0)
        att.append(
            heads(q[own], keys, values, lanes[...], marks[e][:144] * lanes[2:3], marks[e])
        )
    hr[...], hl[...] = halves_of(wide + normed(dot(jnp.concatenate(att, axis=0), out[...])))


def feed_one(h, expand, shrink):
    grown = gelu(dot(h, expand[...])).astype(BF)
    return (h.astype(F32) + normed(dot(grown, shrink[...]))).astype(BF)


def feed_kernel(h1, h2, expand, shrink, out1, out2):
    out1[...] = feed_one(h1[...], expand, shrink)
    out2[...] = feed_one(h2[...], expand, shrink)


def feed_some_kernel(h, expand, shrink, out):
    out[...] = feed_one(h[...], expand, shrink)


def merge_kernel(l1, l2, r1, r2, pm, weight, coarse, ball, *, g):
    for half, (one, two) in enumerate(((l1, l2), (r1, r2))):
        for n, block in enumerate((two[144:], (one[:144], one[144:])[g], (one[144:], two[:144])[g])):
            ball[288 * n + half * 144:288 * n + half * 144 + 144] = block
    picked = dot(pm[g], ball[...])
    quartet = jnp.concatenate([picked[m * 144:m * 144 + 144] for m in range(4)], axis=1)
    coarse[...] = dot(normed(quartet).astype(BF), weight[...]).astype(BF)


def skip_kernel(l1, l2, r1, r2, perm, skip):
    for half, (one, two) in enumerate(((l1, l2), (r1, r2))):
        own = jnp.concatenate([two[144:], one[...], two[:144]], axis=0)
        got = dot(perm[...], own).astype(BF)
        for l in range(4):
            at = l * 288 + half * 144
            skip[at:at + 144] = got[l * 144:l * 144 + 144]


def attend_two_kernel(me, own, other, w3, ones, lanes, srow, x_out, att_out):
    a, b = own[...].astype(F32), other[...].astype(F32)
    first = me[0] == 0
    t0, t1 = jnp.where(first, a, b), jnp.where(first, b, a)
    x = jnp.concatenate([t0[:72], t1[:72], t0[72:], t1[72:]], axis=0).astype(BF)
    x_out[...] = x
    q = unit(dot_nt(x, w3[0]).astype(BF), ones[...], srow[...])
    k = unit(dot_nt(x, w3[1]).astype(BF), ones[...])
    v = dot_nt(x, w3[2]).astype(BF)
    for lg in range(2):
        span = slice(lg * 144, lg * 144 + 144)
        att_out[span] = heads(q[span], k[span], v[span], lanes[...])


def feed_two_kernel(me, x, mine, theirs, o_mine, o_theirs, expand, shrink, keep, send, hid_own):
    branch = dot(mine[...], o_mine[...]) + dot(theirs[...], o_theirs[...])
    hid = (x[...].astype(F32) + normed(branch)).astype(BF)
    acc = dot(gelu(dot_nt(hid, expand[...])).astype(BF), shrink[...])
    first = me[0] == 0

    def split(values):
        p0 = jnp.concatenate([values[0:72], values[144:216]], axis=0)
        p1 = jnp.concatenate([values[72:144], values[216:288]], axis=0)
        return jnp.where(first, p0, p1), jnp.where(first, p1, p0)

    own, far = split(acc)
    keep[...] = own
    send[...] = far.astype(BF)
    hid_own[...] = split(hid.astype(F32))[0].astype(BF)


def finish_rows(k, r, h, pout):
    done = (h[...].astype(F32) + normed(k[...] + r[...].astype(F32))).astype(BF)
    return dot(pout[...], done).reshape(6, 6, 4, 1024).astype(BF)


def finish_first_kernel(k, r, h, pout, rows):
    rows[...] = finish_rows(k, r, h, pout)


def finish_kernel(first, k, r, h, pout, coarse):
    coarse[:6] = first[...]
    coarse[6:] = finish_rows(k, r, h, pout)


def behind(value, axis, steps):
    count = lax.axis_size(axis)
    return lax.ppermute(value, axis, [(s, (s + steps) % count) for s in range(count)])


def after(value, done):
    return lax.optimization_barrier((value, done))[0]


def across(value, axis, flip):
    return lax.ppermute(value, axis, [(s, s ^ flip) for s in range(lax.axis_size(axis))])


def shards(
    patches,
    region_ids,
    triple_one,
    output_one,
    expand_one,
    shrink_one,
    scales_one,
    merge_weight,
    triple_two,
    output_two,
    expand_two,
    shrink_two,
    scales_two,
):
    me = lax.axis_index("tp").astype(jnp.int32).reshape(1)
    lat_at = (lax.axis_index("lat") & 3).astype(jnp.int32).reshape(1)
    ones = const(np.kron(np.eye(4), np.ones((64, 64))))
    lane_of = np.zeros((8, 128), np.float32)
    lane_of[0, :64] = 1
    lane_of[1, 64:] = 1
    lane_of[2] = MASK
    lane_of[2, 8] = -MASK
    lanes = const(lane_of)
    spread = const(np.kron(np.eye(8), np.ones((1, 64))))
    col_axes = ("lon", "tp")
    tok = lambda n: ((n, 512), BF)

    home = patches.transpose(0, 2, 1, 3).reshape(4, 2, 144, 512)
    left = call(pack_kernel, [tok(576)], [home[:, 0]], 10**8)[0]
    right = call(pack_kernel, [tok(576)], [after(home, left)[:, 1]], 10**9)[0]
    region_ids = after(region_ids, right)
    left = behind(left, col_axes, -1)
    pick, keep = pick_rows()
    classes, s_one, s_two, quarter = call(
        ready_kernel,
        [((1152, 128), BF), ((1, 512), F32), ((1, 512), F32), ((128, 1024), BF)],
        [
            lat_at,
            region_ids.transpose(2, 0, 1),
            const(pick),
            const(keep),
            scales_one.reshape(1, 8),
            scales_two.reshape(1, 8),
            spread,
            output_two,
        ],
        10**9,
        smem=(0,),
        hbm=(7,),
        scratch=[pltpu.SemaphoreType.DMA],
    )
    quarter = after(quarter, left)
    oa = behind(quarter, "tp", 1)
    down, up = call(rim_kernel, [tok(216), tok(144)], [left, right, classes], 10**6)
    classes = after(classes, down)
    down, up = behind(down, "lat", 1), behind(up, "lat", -1)

    w_one = triple_one.transpose(1, 0, 2)
    shared = [classes, w_one, output_one, ones, lanes, s_one]
    hr1, hl1 = call(first_kernel, [tok(288)] * 2, [right, left] + shared, 4 * 10**9)
    hl1 = behind(hl1, col_axes, 1)
    shared[0] = after(classes, (hr1, oa))
    hr2, hl2 = call(
        second_kernel, [tok(288)] * 2, [right, left, down, up] + shared, 6 * 10**9
    )
    hl2 = behind(hl2, col_axes, 1)

    feeds = [expand_one, shrink_one]
    br1, br2 = call(feed_kernel, [tok(288)] * 2, [hr1, hr2] + feeds, 3 * 10**9)
    bl1 = call(feed_some_kernel, [tok(288)], [after(hl1, br1)] + feeds, 2 * 10**9)[0]
    oa = after(oa, bl1)
    ob, oc = across(oa, "lat", 1), across(oa, "lat", 2)
    bl2 = call(feed_some_kernel, [tok(288)], [after(hl2, bl1)] + feeds, 2 * 10**9)[0]
    blocks = [bl1, bl2, br1, br2]
    od = across(after(oc, bl2), "lat", 1)
    pm, coarse_in = const(merge_rows()), []
    for g in range(2):
        if g:
            blocks = [after(blocks[0], coarse_in[0])] + blocks[1:]
        coarse_in += call(
            functools.partial(merge_kernel, g=g),
            [((144, 1024), BF)],
            blocks + [pm, merge_weight],
            10**9,
            scratch=[pltpu.VMEM((864, 512), BF)],
        )
    c0, c1 = coarse_in
    d0, d1 = behind(c0, "tp", 1), behind(c1, "tp", 1)
    blocks[0], od = after(blocks[0], c1), after(od, c1)
    skip = call(skip_kernel, [tok(1152)], blocks + [const(home_rows())], 2 * 10**9)[0]
    o_theirs = call(
        join_kernel, [((512, 1024), BF)], [lat_at, oa, ob, oc, od], 10**9, smem=(0,)
    )[0]
    c0, skip, o_theirs = lax.optimization_barrier((c0, skip, o_theirs))
    skip = skip.reshape(4, 12, 24, 512).transpose(0, 2, 1, 3)

    w_two = triple_two.transpose(1, 0, 2)
    attended = []
    for own, other in ((c0, d0), (c1, d1)):
        if attended:
            own = after(own, attended[0][1])
        x, mine = call(
            attend_two_kernel,
            [((288, 1024), BF), tok(288)],
            [me, own, other, w_two, ones, lanes, s_two],
            2 * 10**9,
            smem=(0,),
        )
        attended.append((x, mine, behind(mine, "tp", 1)))
    kept = []
    for x, mine, theirs in attended:
        if kept:
            x = after(x, kept[0][0])
        keep, send, hid_own = call(
            feed_two_kernel,
            [((144, 1024), F32), ((144, 1024), BF), ((144, 1024), BF)],
            [me, x, mine, theirs, output_two, o_theirs, expand_two, shrink_two],
            10**8,
            smem=(0,),
        )
        kept.append((keep, behind(send, "tp", 1), hid_own))
    pout = const(coarse_rows())
    first = call(finish_first_kernel, [((6, 6, 4, 1024), BF)], [*kept[0], pout], 10**8)[0]
    coarse = call(finish_kernel, [((12, 6, 4, 1024), BF)], [first, *kept[1], pout], 10**8)[0]
    return (skip, coarse.transpose(2, 0, 1, 3))


def solution(mesh):
    in_specs = (
        P(None, "lat", ("lon", "tp"), None),
        P(None, "lat", ("lon", "tp")),
        P(),
        P(),
        P(),
        P(),
        P(),
        P(),
        P("tp", None, None),
        P("tp", None),
        P("tp", None),
        P("tp", None),
        P("tp"),
    )
    out_specs = (P(None, "lat", ("lon", "tp"), None), P(None, "lat", ("lon", "tp"), None))
    return jax.shard_map(shards, mesh=mesh, in_specs=in_specs, out_specs=out_specs, check_vma=False)
```
